32 devices in a mesh: groups: 2 (over x), wide: 16 (over z, y, core).
Axes of the slice: x: 2, y: 2, z: 4, core: 2. Of those that a mesh axis runs over, the one named last changes fastest.
Arguments:
- root_band: bfloat16 [128, 2, 48, 384], P(('groups', 'wide')), parts along dimension 0, may hold values from -3 to 3
- w_one: bfloat16 [128, 2, 96, 384], P(('groups', 'wide')), parts along dimension 0, may hold values from -0.21875 to 0.21875
- e_one: bfloat16 [128, 2, 96, 384], P(('groups', 'wide')), parts along dimension 0, may hold values from -3 to 3
- w_two: bfloat16 [128, 2, 384, 384], P(('groups', 'wide')), parts along dimension 0, may hold values from -0.15625 to 0.15625
- e_two: bfloat16 [128, 2, 192, 384], P(('groups', 'wide')), parts along dimension 0, may hold values from -3 to 3
- w_three: bfloat16 [128, 2, 1152, 384], P(('groups', 'wide')), parts along dimension 0, may hold values from -0.125 to 0.125
- e_three: bfloat16 [128, 2, 384, 384], P(('groups', 'wide')), parts along dimension 0, may hold values from -3 to 3
- mask_one: int32 [4, 3, 3], P('groups'), parts along dimension 0, may hold values 0 or 1
- mask_two: int32 [8, 6, 3], P('groups'), parts along dimension 0, may hold values 0 or 1
- mask_three: int32 [16, 9, 3], P('groups'), parts along dimension 0, may hold values 0 or 1
- pole_weights: float32 [8, 2], replicated, may hold values from -3 to 3
Outputs:
- density: float32 [24576, 384], P(('groups', 'wide')), parts along dimension 0
The draws below stay inside these ranges and needn't reach their ends.
There are 2 independent parts, one for each index of `groups`. The reference program is written for one: setup_inputs(seed, part) draws one part's arguments, and reference() takes and returns one part's arrays. A program takes and returns all parts, laid end to end along the dimension named above; an argument that names none is the same for every part. Nothing has to cross between parts.
All inputs are finite; a program needn't handle non-finite values.
Results may differ from the reference program's by a relative error of at most 0.0032.
Values may be sent and summed in bfloat16 or wider, within the bound.
No kernel may reach another device: no remote copies, remote signals or barrier semaphores. Data moves between devices by JAX's collectives and lax.ppermute only.
A program may use at most 192 MiB of HBM per device.

```python
import jax
import jax.numpy as jnp
from jax import lax

POLES = 8
SEP = 3
SB = 384


def plant(values, key, smallest, largest):
    longest = values.shape.index(max(values.shape))
    spots = []
    for shift in (0, 1):
        where = [jax.random.randint(jax.random.fold_in(key, axis), (), 0, length) for axis, length in enumerate(values.shape)]
        where[longest] = (where[longest] + shift) % values.shape[longest]
        spots.append(tuple(where))
    return values.at[spots[0]].set(smallest).at[spots[1]].set(largest)


def level_of(rng, shape, split, low, largest):
    def one(axis_at, parts):
        steps = jax.random.uniform(jax.random.fold_in(jax.random.fold_in(rng, 6), axis_at), (parts,), jnp.float32, low / len(split), largest / len(split))
        return jnp.repeat(jnp.exp(steps), shape[axis_at] // parts).reshape((-1,) + (1,) * (len(shape) - axis_at - 1))

    gain = one(*split[0])
    for cut in split[1:]:
        gain = gain * one(*cut)
    return gain


def normal_values(key, shape, deviation, most, cuts=(), kind=jnp.bfloat16):
    gain = level_of(key, shape, cuts, -0.22, 0.18) if cuts else 1.0
    values = jax.random.normal(key, shape, jnp.float32) * deviation * gain
    return jnp.minimum(jnp.maximum(values, -most), most).astype(kind)


def setup_inputs(seed: int = 0, part: int = 0) -> dict:
    arg_keys = jax.random.split(jax.random.key(seed), 12)
    own_keys = jax.random.split(jax.random.fold_in(arg_keys[11], part), 12)
    return {
        "root_band": normal_values(own_keys[0], (8 * POLES, 2, SB // 8, SB), 0.5, 3.0, ((0, 16),)),
        "w_one": normal_values(own_keys[1], (8 * POLES, 2, SB // 4, SB), (2 * SB) ** -0.5, 0.21875, ((0, 16),)),
        "e_one": normal_values(own_keys[2], (8 * POLES, 2, SB // 4, SB), 0.5, 3.0, ((0, 16),)),
        "w_two": normal_values(own_keys[3], (8 * POLES, 2, SB, SB), (4 * SB) ** -0.5, 0.15625, ((0, 16),)),
        "e_two": normal_values(own_keys[4], (8 * POLES, 2, SB // 2, SB), 0.5, 3.0, ((0, 16),)),
        "w_three": normal_values(own_keys[5], (8 * POLES, 2, 3 * SB, SB), (6 * SB) ** -0.5, 0.125, ((0, 16),)),
        "e_three": normal_values(own_keys[6], (8 * POLES, 2, SB, SB), 0.5, 3.0, ((0, 16),)),
        "mask_one": plant((jax.random.randint(own_keys[7], (2, SEP, SEP), 0, 2) < 1).astype(jnp.int32), jax.random.fold_in(own_keys[7], 1), 0, 1),
        "mask_two": plant((jax.random.randint(own_keys[8], (4, 2 * SEP, SEP), 0, 4) < 3).astype(jnp.int32), jax.random.fold_in(own_keys[8], 1), 0, 1),
        "mask_three": plant((jax.random.randint(own_keys[9], (8, 3 * SEP, SEP), 0, 4) < 3).astype(jnp.int32), jax.random.fold_in(own_keys[9], 1), 0, 1),
        "pole_weights": normal_values(arg_keys[10], (POLES, 2), 0.5, 3.0, (), jnp.float32),
    }


def complex_dot(left, right):
    first = left.astype(jnp.float32)
    second = right.astype(jnp.float32)

    def single(alpha, beta):
        return jnp.dot(alpha, beta, precision=lax.Precision.HIGHEST, preferred_element_type=jnp.float32)

    real_part = single(first[0], second[0]) - single(first[1], second[1])
    imag_part = single(first[0], second[1]) + single(first[1], second[0])
    return jnp.stack([real_part, imag_part])


def complex_tdot(left, right):
    return complex_dot(jnp.swapaxes(left, 1, 2), right)


def with_pattern(panel, tiles):
    extent = panel.shape[-1] // tiles.shape[-1]
    spread = jnp.repeat(jnp.repeat(tiles, extent, axis=0), extent, axis=1)
    return panel * spread.astype(panel.dtype)[None]


def extend_path(path, coupling, corner):
    negated = -coupling
    upper_rows = jnp.concatenate([path, negated], axis=2)
    lower_rows = jnp.concatenate([jnp.swapaxes(negated, 1, 2), corner], axis=2)
    return jnp.concatenate([upper_rows, lower_rows], axis=1)


def rounded(value):
    return lax.optimization_barrier(value.astype(jnp.bfloat16))


def reference(root_band, w_one, e_one, w_two, e_two, w_three, e_three, mask_one, mask_two, mask_three, pole_weights):
    root_full = root_band.reshape(8, POLES, 2, SB // 8, SB).transpose(1, 2, 0, 3, 4).reshape(POLES, 2, SB, SB)
    panel_one = w_one.reshape(2, 4, POLES, 2, SB // 4, SB).transpose(2, 0, 3, 1, 4, 5).reshape(POLES, 2, 2, SB, SB)
    block_one = e_one.reshape(2, 4, POLES, 2, SB // 4, SB).transpose(2, 0, 3, 1, 4, 5).reshape(POLES, 2, 2, SB, SB)
    panel_two = w_two.reshape(4, 2, POLES, 2, SB, SB).transpose(2, 0, 3, 1, 4, 5).reshape(POLES, 4, 2, 2 * SB, SB)
    block_two = e_two.reshape(4, 2, POLES, 2, SB // 2, SB).transpose(2, 0, 3, 1, 4, 5).reshape(POLES, 4, 2, SB, SB)
    panel_three = w_three.reshape(8, POLES, 2, 3 * SB, SB).transpose(1, 0, 2, 3, 4)
    block_three = e_three.reshape(8, POLES, 2, SB, SB).transpose(1, 0, 2, 3, 4)

    def one_pole(density, inputs):
        root, pan_one, blk_one, pan_two, blk_two, pan_three, blk_three, weight = inputs
        level_one = []
        for branch in range(2):
            masked = with_pattern(pan_one[branch], mask_one[branch])
            coupling = rounded(complex_dot(root, masked))
            corner = rounded(blk_one[branch].astype(jnp.float32) + complex_tdot(masked, coupling))
            level_one.append(extend_path(root, coupling, corner))
        level_two = []
        for branch in range(4):
            masked = with_pattern(pan_two[branch], mask_two[branch])
            coupling = rounded(complex_dot(level_one[branch // 2], masked))
            corner = rounded(blk_two[branch].astype(jnp.float32) + complex_tdot(masked, coupling))
            level_two.append(extend_path(level_one[branch // 2], coupling, corner))
        columns = []
        for branch in range(8):
            masked = with_pattern(pan_three[branch], mask_three[branch])
            coupling = complex_dot(level_two[branch // 2], masked)
            coupling_low = rounded(coupling)
            corner = blk_three[branch].astype(jnp.float32) + complex_tdot(masked, coupling_low)
            column = jnp.concatenate([-coupling, corner], axis=1)
            columns.append(weight[0] * column[1] + weight[1] * column[0])
        return density + jnp.stack(columns), None

    start = jnp.zeros((8, 4 * SB, SB), jnp.float32)
    density, unused = lax.scan(one_pole, start, (root_full, panel_one, block_one, panel_two, block_two, panel_three, block_three, pole_weights.astype(jnp.float32)))
    return density.reshape(32 * SB, SB)
```

```python
import functools

import jax
import jax.numpy as jnp
from jax import lax
from jax.experimental import pallas as pl
from jax.experimental.pallas import tpu as pltpu
from jax.sharding import PartitionSpec as P

BF16 = jnp.bfloat16
F32 = jnp.float32


def mask_row(mask_ref, first, extent, width):
    lane = lax.broadcasted_iota(jnp.int32, (1, width), 1)
    row = jnp.zeros((1, width), F32)
    for column in range(width // extent):
        value = mask_ref[first + column].astype(F32)
        inside = (lane >= column * extent) & (lane < (column + 1) * extent)
        row = jnp.where(inside, value, row)
    return row.astype(BF16)


def pack_right(target, block, rows, real, imag, sb):
    low = 2 * sb * block + rows.start
    count = rows.stop - rows.start
    target[low : low + count, 0:sb] = real
    target[low : low + count, sb : 2 * sb] = imag
    target[low + sb : low + sb + count, 0:sb] = -imag
    target[low + sb : low + sb + count, sb : 2 * sb] = real


def mask_panel(raw, mask_ref, base, right, turned, sb, extent):
    columns = sb // extent
    for tile in range(raw.shape[1] // extent):
        row = mask_row(mask_ref, base + tile * columns, extent, sb)
        rows = slice(tile * extent, (tile + 1) * extent)
        real = raw[0, rows, :] * row
        imag = raw[1, rows, :] * row
        block = tile // columns
        inner = slice((tile % columns) * extent, (tile % columns + 1) * extent)
        pack_right(right, block, inner, real, imag, sb)
        low = 2 * sb * block + inner.start
        turned[:, low : low + extent] = real.T
        turned[:, low + sb : low + sb + extent] = imag.T


def dot(left, right):
    return jnp.dot(left, right, preferred_element_type=F32)


def couple(path, right, packed, level, sb):
    size = 2 * sb * level
    for block in range(level):
        rows = slice(block * sb, (block + 1) * sb)
        product = dot(path[rows, 0:size], right[...]).astype(BF16)
        real, imag = product[:, 0:sb], product[:, sb : 2 * sb]
        path[rows, size : size + 2 * sb] = -product
        pack_right(packed, block, slice(0, sb), real, imag, sb)
        low = 2 * sb * block
        path[level * sb : (level + 1) * sb, low : low + sb] = -real.T
        path[level * sb : (level + 1) * sb, low + sb : low + 2 * sb] = -imag.T


def close(path, turned, packed, corner, level, sb):
    size = 2 * sb * level
    product = dot(turned[...], packed[...])
    rows = slice(level * sb, (level + 1) * sb)
    for part in range(2):
        own = product[:, part * sb : (part + 1) * sb] + corner[part].astype(F32)
        path[rows, size + part * sb : size + (part + 1) * sb] = own.astype(BF16)


def pole_kernel(pole, local, first, sb, extent, *refs):
    place, mask_one, mask_two, mask_three, weights = refs[:5]
    roots = refs[5:13]
    ones = refs[13:17]
    twos = refs[17:19]
    corners = refs[19:21]
    w_three, e_three = refs[21:23]
    rest = refs[23:]
    if first:
        total_in = None
    else:
        total_in, rest = rest[0], rest[1:]
    (out, path, w1, e1, w2, e2, w3, e3, m1, m1t, m2, m2t, m3, m3t, x1, x2, x3, sems) = rest
    leaf = place[0]
    member = place[1]
    band, quarter, half = sb // 8, sb // 4, sb // 2
    copies = {}
    count = [0]

    def begin(name, source, target):
        copy = pltpu.make_async_copy(source, target, sems.at[count[0]])
        count[0] += 1
        copy.start()
        copies.setdefault(name, []).append(copy)

    def finish(*names):
        for name in names:
            for copy in copies[name]:
                copy.wait()

    def at(index, size):
        return pl.ds(pl.multiple_of(index * size, size), size)

    for turn in range(8):
        rows = at(leaf ^ turn, band)
        for part in range(2):
            begin("e0", roots[turn].at[pole, part], path.at[rows, part * sb : (part + 1) * sb])
    for turn in range(4):
        rows = at((leaf & 3) ^ turn, quarter)
        begin("w1", ones[turn].at[:, 0:quarter, :], w1.at[:, rows, :])
        begin("w1", ones[turn].at[:, quarter : 2 * quarter, :], e1.at[:, rows, :])
    begin("w3", w_three.at[pole], w3)
    for turn in range(2):
        begin("w2", twos[turn], w2.at[:, at((leaf & 1) ^ turn, sb), :])
    for turn in range(2):
        begin("e2", corners[turn], e2.at[:, at((leaf & 1) ^ turn, half), :])
    begin("e3", e_three.at[pole], e3)
    if total_in is not None:
        begin("total", total_in, out)
    weight_imag = weights[2 * (member * local + pole)]
    weight_real = weights[2 * (member * local + pole) + 1]

    columns = sb // extent
    tiles = columns * columns
    finish("e0", "w1")
    mask_panel(w1, mask_one, (leaf >> 2) * tiles, m1, m1t, sb, extent)
    couple(path, m1, x1, 1, sb)
    finish("w3", "w2", "e2", "e3")
    mask_panel(w2, mask_two, (leaf >> 1) * 2 * tiles, m2, m2t, sb, extent)
    close(path, m1t, x1, e1, 1, sb)
    mask_panel(w3, mask_three, leaf * 3 * tiles, m3, m3t, sb, extent)
    couple(path, m2, x2, 2, sb)
    close(path, m2t, x2, e2, 2, sb)
    if total_in is not None:
        finish("total")

    def add_rows(rows, value):
        if total_in is None:
            out[rows, :] = value
        else:
            out[rows, :] = out[rows, :] + value

    for block in range(3):
        rows = slice(block * sb, (block + 1) * sb)
        product = dot(path[rows, :], m3[...])
        real, imag = product[:, 0:sb], product[:, sb : 2 * sb]
        add_rows(rows, -(weight_imag * imag + weight_real * real))
        pack_right(x3, block, slice(0, sb), real.astype(BF16), imag.astype(BF16), sb)
    product = dot(m3t[...], x3[...])
    real = product[:, 0:sb] + e3[0].astype(F32)
    imag = product[:, sb : 2 * sb] + e3[1].astype(F32)
    add_rows(slice(3 * sb, 4 * sb), weight_imag * imag + weight_real * real)


def run_pole(pole, local, scalars, roots, ones, twos, corners, w_three, e_three, total):
    sb = w_three.shape[-1]
    extent = scalars[5]
    first = total is None
    operands = [*scalars[:5], *roots, *ones, *twos, *corners, w_three, e_three]
    if not first:
        operands.append(total)
    smem = pl.BlockSpec(memory_space=pltpu.SMEM)
    anywhere = pl.BlockSpec(memory_space=pl.ANY)
    vmem = lambda *shape: pltpu.VMEM(shape, BF16)
    return pl.pallas_call(
        functools.partial(pole_kernel, pole, local, first, sb, extent),
        out_shape=jax.ShapeDtypeStruct((4 * sb, sb), F32),
        in_specs=[smem] * 5 + [anywhere] * (len(operands) - 5),
        out_specs=pl.BlockSpec(memory_space=pltpu.VMEM),
        scratch_shapes=[
            vmem(3 * sb, 6 * sb),
            vmem(2, sb, sb),
            vmem(2, sb, sb),
            vmem(2, 2 * sb, sb),
            vmem(2, sb, sb),
            vmem(2, 3 * sb, sb),
            vmem(2, sb, sb),
            vmem(2 * sb, 2 * sb),
            vmem(sb, 2 * sb),
            vmem(4 * sb, 2 * sb),
            vmem(sb, 4 * sb),
            vmem(6 * sb, 2 * sb),
            vmem(sb, 6 * sb),
            vmem(2 * sb, 2 * sb),
            vmem(4 * sb, 2 * sb),
            vmem(6 * sb, 2 * sb),
            pltpu.SemaphoreType.DMA((32,)),
        ],
        compiler_params=pltpu.CompilerParams(vmem_limit_bytes=56 * 1024 * 1024),
        cost_estimate=pl.CostEstimate(
            flops=160 * sb**3, bytes_accessed=80 * sb * sb, transcendentals=0
        ),
        name="pole_" + str(pole),
    )(*operands)


def shards(
    root_band,
    w_one,
    e_one,
    w_two,
    e_two,
    w_three,
    e_three,
    mask_one,
    mask_two,
    mask_three,
    pole_weights,
):
    devices = lax.axis_size("wide")
    per_leaf = devices // 8
    device_index = lax.axis_index("wide")
    leaf = device_index // per_leaf
    member = device_index % per_leaf
    local = root_band.shape[0]
    sb = w_three.shape[-1]

    def turn(block, bits):
        route = [(low, low ^ bits * per_leaf) for low in range(devices)]
        return lax.ppermute(block, "wide", route)

    roots = {0: root_band, 1: turn(root_band, 1)}
    for bits in (2, 4, 6):
        roots[bits] = turn(root_band, bits)
    ones = []
    for pole in range(local):
        own = jnp.concatenate([w_one[pole], e_one[pole]], axis=1)
        ones.append({0: own, 1: turn(own, 1), 2: turn(own, 2)})
    for bits in (2, 4, 6):
        roots[bits + 1] = turn(roots[1], bits)
    for pole in range(local):
        ones[pole][3] = turn(ones[pole][1], 2)
    twos, corners = [], []
    for pole in range(local):
        twos.append([w_two[pole], turn(w_two[pole], 1)])
        corners.append([e_two[pole], turn(e_two[pole], 1)])

    scalars = (
        jnp.stack([leaf, member]).astype(jnp.int32),
        mask_one.reshape(-1),
        mask_two.reshape(-1),
        mask_three.reshape(-1),
        pole_weights.reshape(-1),
        sb // mask_one.shape[-1],
    )
    density = None
    for pole in range(local):
        density = run_pole(
            pole,
            local,
            scalars,
            [roots[bits] for bits in range(8)],
            [ones[pole][bits] for bits in range(4)],
            twos[pole],
            corners[pole],
            w_three,
            e_three,
            density,
        )
    for level_bit in range(per_leaf.bit_length() - 2, -1, -1):
        half_count = density.shape[0] // 2
        lower_rows = density[:half_count]
        upper_rows = density[half_count:]
        bit_set = member // (1 << level_bit) % 2 == 1
        kept_rows = jnp.where(bit_set, upper_rows, lower_rows)
        sent_rows = jnp.where(bit_set, lower_rows, upper_rows)
        route = [(low, low ^ 1 << level_bit) for low in range(devices)]
        density = kept_rows + lax.ppermute(sent_rows, "wide", route)
    return density


def solution(mesh):
    split = P(("groups", "wide"), None, None, None)
    return jax.shard_map(
        shards,
        mesh=mesh,
        in_specs=(split,) * 7 + (P("groups", None, None),) * 3 + (P(),),
        out_specs=P(("groups", "wide"), None),
        check_vma=False,
    )
```

```python
import functools

import jax
import jax.numpy as jnp
from jax import lax
from jax.experimental import pallas as pl
from jax.experimental.pallas import tpu as pltpu
from jax.sharding import PartitionSpec as P

BF16 = jnp.bfloat16
F32 = jnp.float32


def mask_row(mask_ref, tile, extent, width):
    lane = lax.broadcasted_iota(jnp.int32, (1, width), 1)
    row = jnp.zeros((1, width), F32)
    for column in range(width // extent):
        value = mask_ref[tile, column].astype(F32)
        inside = (lane >= column * extent) & (lane < (column + 1) * extent)
        row = jnp.where(inside, value, row)
    return row.astype(BF16)


def pack_right(target, block, rows, real, imag, sb):
    low = 2 * sb * block + rows.start
    count = rows.stop - rows.start
    target[low : low + count, 0:sb] = real
    target[low : low + count, sb : 2 * sb] = imag
    target[low + sb : low + sb + count, 0:sb] = -imag
    target[low + sb : low + sb + count, sb : 2 * sb] = real


def mask_panel(raw, mask_ref, base, right, turned, sb, extent):
    columns = sb // extent
    for tile in range(raw.shape[1] // extent):
        row = mask_row(mask_ref, base + tile, extent, sb)
        rows = slice(tile * extent, (tile + 1) * extent)
        real = raw[0, rows, :] * row
        imag = raw[1, rows, :] * row
        block = tile // columns
        inner = slice((tile % columns) * extent, (tile % columns + 1) * extent)
        pack_right(right, block, inner, real, imag, sb)
        low = 2 * sb * block + inner.start
        turned[:, low : low + extent] = real.T
        turned[:, low + sb : low + sb + extent] = imag.T


def dot(left, right):
    return jnp.dot(left, right, preferred_element_type=F32)


def row_products(path, right, size, level, whole, sb):
    if whole:
        product = dot(path[0 : level * sb, 0:size], right[...])
        for block in range(level):
            yield block, product[block * sb : (block + 1) * sb, :]
    else:
        for block in range(level):
            yield block, dot(path[block * sb : (block + 1) * sb, 0:size], right[...])


def couple(path, right, packed, level, whole, sb):
    size = 2 * sb * level
    for block, product in row_products(path, right, size, level, whole, sb):
        rows = slice(block * sb, (block + 1) * sb)
        product = product.astype(BF16)
        real, imag = product[:, 0:sb], product[:, sb : 2 * sb]
        path[rows, size : size + 2 * sb] = -product
        pack_right(packed, block, slice(0, sb), real, imag, sb)
        low = 2 * sb * block
        path[level * sb : (level + 1) * sb, low : low + sb] = -real.T
        path[level * sb : (level + 1) * sb, low + sb : low + 2 * sb] = -imag.T


def close(path, turned, packed, corner, level, sb):
    size = 2 * sb * level
    product = dot(turned[...], packed[...])
    rows = slice(level * sb, (level + 1) * sb)
    for part in range(2):
        own = product[:, part * sb : (part + 1) * sb] + corner[part].astype(F32)
        path[rows, size + part * sb : size + (part + 1) * sb] = own.astype(BF16)


def pole_kernel(pole, local, per_leaf, whole, places, sb, extent, *refs):
    masks, weights = refs[:2]
    sources, rest = refs[2:-18], refs[-18:]
    (out, path, w1, e1, w2, e2, w3, e3, m1, m1t, m2, m2t, m3, m3t, x1, x2, x3, sems) = rest
    device = lax.axis_index("wide")
    leaf = device // per_leaf
    member = device % per_leaf
    band, quarter, half = sb // 8, sb // 4, sb // 2
    copies = {}
    count = [0]

    def begin(name, source, target):
        copy = pltpu.make_async_copy(source, target, sems.at[count[0]])
        count[0] += 1
        copy.start()
        copies.setdefault(name, []).append(copy)

    def finish(*names):
        for name in names:
            for copy in copies[name]:
                copy.wait()

    def at(index, size):
        return pl.ds(pl.multiple_of(index * size, size), size)

    def views(name, index):
        operand, where, low, high = places[name][index]
        source = sources[operand]
        if where is not None:
            source = source.at[where]
        return source if low is None else source.at[:, low:high, :]

    for turn in range(8):
        rows = at(leaf ^ turn, band)
        source = views("root", turn)
        for part in range(2):
            begin("e0", source.at[part], path.at[rows, part * sb : (part + 1) * sb])
    for turn in range(4):
        rows = at((leaf & 3) ^ turn, quarter)
        begin("w1", views("w_one", turn), w1.at[:, rows, :])
        begin("w1", views("e_one", turn), e1.at[:, rows, :])
    begin("w3", views("w_three", 0), w3)
    for turn in range(2):
        begin("w2", views("w_two", turn), w2.at[:, at((leaf & 1) ^ turn, sb), :])
    for turn in range(2):
        begin("e2", views("e_two", turn), e2.at[:, at((leaf & 1) ^ turn, half), :])
    begin("e3", views("e_three", 0), e3)
    first = "total" not in places
    if not first:
        begin("total", sources[places["total"]], out)
    weight_imag = weights[member * local + pole, 0]
    weight_real = weights[member * local + pole, 1]

    columns = sb // extent
    finish("e0", "w1")
    mask_panel(w1, masks, 0, m1, m1t, sb, extent)
    couple(path, m1, x1, 1, whole, sb)
    finish("w3", "w2", "e2", "e3")
    mask_panel(w2, masks, columns, m2, m2t, sb, extent)
    close(path, m1t, x1, e1, 1, sb)
    mask_panel(w3, masks, 3 * columns, m3, m3t, sb, extent)
    couple(path, m2, x2, 2, whole, sb)
    close(path, m2t, x2, e2, 2, sb)
    if not first:
        finish("total")

    def add_rows(rows, value):
        if first:
            out[rows, :] = value
        else:
            out[rows, :] = out[rows, :] + value

    for block, product in row_products(path, m3, 6 * sb, 3, whole, sb):
        rows = slice(block * sb, (block + 1) * sb)
        real, imag = product[:, 0:sb], product[:, sb : 2 * sb]
        add_rows(rows, -(weight_imag * imag + weight_real * real))
        pack_right(x3, block, slice(0, sb), real.astype(BF16), imag.astype(BF16), sb)
    product = dot(m3t[...], x3[...])
    real = product[:, 0:sb] + e3[0].astype(F32)
    imag = product[:, sb : 2 * sb] + e3[1].astype(F32)
    add_rows(slice(3 * sb, 4 * sb), weight_imag * imag + weight_real * real)


def run_pole(pole, local, per_leaf, whole, masks, weights, pieces, total, sb, extent):
    sources, places = [], {}

    def operand(array):
        for index, known in enumerate(sources):
            if known is array:
                return index
        sources.append(array)
        return len(sources) - 1

    for name, turns in pieces.items():
        places[name] = {turn: (operand(piece[0]), *piece[1:]) for turn, piece in turns.items()}
    if total is not None:
        places["total"] = operand(total)
    operands = [masks, weights, *sources]
    smem = pl.BlockSpec(memory_space=pltpu.SMEM)
    anywhere = pl.BlockSpec(memory_space=pl.ANY)
    vmem = lambda *shape: pltpu.VMEM(shape, BF16)
    return pl.pallas_call(
        functools.partial(pole_kernel, pole, local, per_leaf, whole, places, sb, extent),
        out_shape=jax.ShapeDtypeStruct((4 * sb, sb), F32),
        in_specs=[smem] * 2 + [anywhere] * len(sources),
        out_specs=pl.BlockSpec(memory_space=pltpu.VMEM),
        scratch_shapes=[
            vmem(3 * sb, 6 * sb),
            vmem(2, sb, sb),
            vmem(2, sb, sb),
            vmem(2, 2 * sb, sb),
            vmem(2, sb, sb),
            vmem(2, 3 * sb, sb),
            vmem(2, sb, sb),
            vmem(2 * sb, 2 * sb),
            vmem(sb, 2 * sb),
            vmem(4 * sb, 2 * sb),
            vmem(sb, 4 * sb),
            vmem(6 * sb, 2 * sb),
            vmem(sb, 6 * sb),
            vmem(2 * sb, 2 * sb),
            vmem(4 * sb, 2 * sb),
            vmem(6 * sb, 2 * sb),
            pltpu.SemaphoreType.DMA((32,)),
        ],
        compiler_params=pltpu.CompilerParams(vmem_limit_bytes=56 * 1024 * 1024),
        cost_estimate=pl.CostEstimate(
            flops=160 * sb**3, bytes_accessed=80 * sb * sb, transcendentals=0
        ),
        name="pole_" + str(pole),
    )(*operands)


def shards(
    root_band,
    w_one,
    e_one,
    w_two,
    e_two,
    w_three,
    e_three,
    mask_one,
    mask_two,
    mask_three,
    pole_weights,
):
    devices = lax.axis_size("wide")
    per_leaf = devices // 8
    device_index = lax.axis_index("wide")
    leaf = device_index // per_leaf
    member = device_index % per_leaf
    local = root_band.shape[0]
    sb = w_three.shape[-1]
    quarter, half = sb // 4, sb // 2

    def turn(block, bits, after=()):
        if after:
            block = lax.optimization_barrier((block, *after))[0]
        route = [(low, low ^ bits * per_leaf) for low in range(devices)]
        return lax.ppermute(block, "wide", route)

    early = (local + 1) // 2
    batches = [slice(0, early)] + ([slice(early, local)] if local > early else [])
    packs = [jnp.concatenate([w_one[batch], e_one[batch]], axis=2) for batch in batches]
    root_y = turn(root_band, 1)
    one_y = [turn(packs[0], 1)]
    one_z = [turn(packs[0], 2)]
    if len(batches) > 1:
        one_y.append(turn(packs[1], 1))
    root_pair = jnp.concatenate([root_band, root_y], axis=0)
    panels = [jnp.concatenate([w_two[pole], e_two[pole]], axis=1) for pole in range(local - 1)]
    two_y = []
    if local > 1:
        two_y.append(turn(panels[0], 1))
    root_z = {2: turn(root_pair, 2)}
    root_z[4] = turn(root_pair, 4, (one_z[0],))
    root_z[6] = turn(root_pair, 6, (one_y[0],))
    one_yz = [turn(one_y[0], 2, (root_z[2],))]
    if local > 2:
        two_y.append(turn(panels[1], 1, (one_y[1],)))
    if len(batches) > 1:
        one_pair = turn(jnp.concatenate([packs[1], one_y[1]], axis=0), 2, (root_z[4],))
    if local > 3:
        two_y.append(turn(panels[2], 1, (root_z[6],)))
    gate = (two_y[0],) if local > 1 else ()
    last_two_y = turn(w_two[local - 1], 1, gate)
    last_corner_y = turn(e_two[local - 1], 1, (one_yz[0],))

    masks = jnp.concatenate(
        [
            lax.dynamic_index_in_dim(mask_one, leaf // 4, 0, keepdims=False),
            lax.dynamic_index_in_dim(mask_two, leaf // 2, 0, keepdims=False),
            lax.dynamic_index_in_dim(mask_three, leaf, 0, keepdims=False),
        ],
        axis=0,
    )
    density = None
    for pole in range(local):
        pieces = {"root": {0: (root_band, pole, None, None), 1: (root_y, pole, None, None)}}
        for bits in (2, 4, 6):
            pieces["root"][bits] = (root_z[bits], pole, None, None)
            pieces["root"][bits + 1] = (root_z[bits], local + pole, None, None)
        batch = 0 if pole < early else 1
        at = pole - batches[batch].start
        count = batches[batch].stop - batches[batch].start
        if batch == 0:
            far = {2: (one_z[0], at), 3: (one_yz[0], at)}
        else:
            far = {2: (one_pair, at), 3: (one_pair, count + at)}
        others = {1: (one_y[batch], at), **far}
        pieces["w_one"] = {0: (w_one, pole, None, None)}
        pieces["e_one"] = {0: (e_one, pole, None, None)}
        for bits, (array, index) in others.items():
            pieces["w_one"][bits] = (array, index, 0, quarter)
            pieces["e_one"][bits] = (array, index, quarter, 2 * quarter)
        pieces["w_two"] = {0: (w_two, pole, None, None)}
        pieces["e_two"] = {0: (e_two, pole, None, None)}
        if pole < local - 1:
            pieces["w_two"][1] = (two_y[pole], None, 0, sb)
            pieces["e_two"][1] = (two_y[pole], None, sb, sb + half)
        else:
            pieces["w_two"][1] = (last_two_y, None, None, None)
            pieces["e_two"][1] = (last_corner_y, None, None, None)
        pieces["w_three"] = {0: (w_three, pole, None, None)}
        pieces["e_three"] = {0: (e_three, pole, None, None)}
        density = run_pole(
            pole,
            local,
            per_leaf,
            pole % 2 == 1,
            masks,
            pole_weights,
            pieces,
            density,
            sb,
            sb // mask_one.shape[-1],
        )
    for level_bit in range(per_leaf.bit_length() - 2, -1, -1):
        half_count = density.shape[0] // 2
        lower_rows = density[:half_count]
        upper_rows = density[half_count:]
        bit_set = member // (1 << level_bit) % 2 == 1
        kept_rows = jnp.where(bit_set, upper_rows, lower_rows)
        sent_rows = jnp.where(bit_set, lower_rows, upper_rows)
        route = [(low, low ^ 1 << level_bit) for low in range(devices)]
        density = kept_rows + lax.ppermute(sent_rows, "wide", route)
    return density


def solution(mesh):
    split = P(("groups", "wide"), None, None, None)
    return jax.shard_map(
        shards,
        mesh=mesh,
        in_specs=(split,) * 7 + (P("groups", None, None),) * 3 + (P(),),
        out_specs=P(("groups", "wide"), None),
        check_vma=False,
    )
```

```python
import functools

import jax
import jax.numpy as jnp
from jax import lax
from jax.experimental import pallas as pl
from jax.experimental.pallas import tpu as pltpu
from jax.sharding import PartitionSpec as P

BF16 = jnp.bfloat16
F32 = jnp.float32
FORMS = ((384, 256), (192, 768), (128, 256), (384, 768))


def mask_row(mask_ref, tile, extent, width):
    lane = lax.broadcasted_iota(jnp.int32, (1, width), 1)
    row = jnp.zeros((1, width), F32)
    for column in range(width // extent):
        value = mask_ref[tile, column].astype(F32)
        inside = (lane >= column * extent) & (lane < (column + 1) * extent)
        row = jnp.where(inside, value, row)
    return row.astype(BF16)


def pack_right(target, block, rows, real, imag, sb):
    low = 2 * sb * block + rows.start
    count = rows.stop - rows.start
    target[low : low + count, 0:sb] = real
    target[low : low + count, sb : 2 * sb] = imag
    target[low + sb : low + sb + count, 0:sb] = -imag
    target[low + sb : low + sb + count, sb : 2 * sb] = real


def mask_panel(raw, mask_ref, base, right, turned, sb, extent):
    columns = sb // extent
    for tile in range(raw.shape[1] // extent):
        row = mask_row(mask_ref, base + tile, extent, sb)
        rows = slice(tile * extent, (tile + 1) * extent)
        real = raw[0, rows, :] * row
        imag = raw[1, rows, :] * row
        block = tile // columns
        inner = slice((tile % columns) * extent, (tile % columns + 1) * extent)
        pack_right(right, block, inner, real, imag, sb)
        low = 2 * sb * block + inner.start
        turned[:, low : low + extent] = real.T
        turned[:, low + sb : low + sb + extent] = imag.T


def dot(left, right):
    return jnp.dot(left, right, preferred_element_type=F32)


def tiled_dot(left, right, rows, size, form):
    step, width = form
    for low in range(rows.start, rows.stop, step):
        part = left[low : low + step, 0:size]
        yield low, low + step, jnp.concatenate(
            [dot(part, right[:, at : at + width]) for at in range(0, right.shape[1], width)], axis=1
        )


def couple(path, right, packed, level, form, sb):
    size = 2 * sb * level
    for low, high, product in tiled_dot(path, right, slice(0, level * sb), size, form):
        product = product.astype(BF16)
        real, imag = product[:, 0:sb], product[:, sb : 2 * sb]
        path[low:high, size : size + 2 * sb] = -product
        block, inner = low // sb, low % sb
        pack_right(packed, block, slice(inner, inner + high - low), real, imag, sb)
        at = 2 * sb * block + inner
        path[level * sb : (level + 1) * sb, at : at + high - low] = -real.T
        path[level * sb : (level + 1) * sb, at + sb : at + sb + high - low] = -imag.T


def close(path, turned, packed, corner, level, form, sb):
    size = 2 * sb * level
    for low, high, product in tiled_dot(turned, packed, slice(0, sb), size, form):
        rows = slice(level * sb + low, level * sb + high)
        for part in range(2):
            own = product[:, part * sb : (part + 1) * sb] + corner[part, low:high, :].astype(F32)
            path[rows, size + part * sb : size + (part + 1) * sb] = own.astype(BF16)


def pole_kernel(pole, local, per_leaf, form, places, sb, extent, *refs):
    masks, weights = refs[:2]
    sources, rest = refs[2:-18], refs[-18:]
    (out, path, w1, e1, w2, e2, w3, e3, m1, m1t, m2, m2t, m3, m3t, x1, x2, x3, sems) = rest
    device = lax.axis_index("wide")
    leaf = device // per_leaf
    member = device % per_leaf
    band, quarter, half = sb // 8, sb // 4, sb // 2
    copies = {}
    count = [0]

    def begin(name, source, target):
        copy = pltpu.make_async_copy(source, target, sems.at[count[0]])
        count[0] += 1
        copy.start()
        copies.setdefault(name, []).append(copy)

    def finish(*names):
        for name in names:
            for copy in copies[name]:
                copy.wait()

    def at(index, size):
        return pl.ds(pl.multiple_of(index * size, size), size)

    def views(name, index):
        operand, where, low, high = places[name][index]
        source = sources[operand]
        if where is not None:
            source = source.at[where]
        return source if low is None else source.at[:, low:high, :]

    for turn in range(2):
        for level in range(4):
            rows = at(2 * level + ((leaf & 1) ^ turn), band)
            source = views("root", 4 * turn + level)
            for part in range(2):
                begin("e0", source.at[part], path.at[rows, part * sb : (part + 1) * sb])
    for turn in range(2):
        for level in range(2):
            rows = at(2 * level + ((leaf & 1) ^ turn), quarter)
            begin("w1", views("w_one", 2 * turn + level), w1.at[:, rows, :])
            begin("w1", views("e_one", 2 * turn + level), e1.at[:, rows, :])
    begin("w3", views("w_three", 0), w3)
    for turn in range(2):
        begin("w2", views("w_two", turn), w2.at[:, at((leaf & 1) ^ turn, sb), :])
    for turn in range(2):
        begin("e2", views("e_two", turn), e2.at[:, at((leaf & 1) ^ turn, half), :])
    begin("e3", views("e_three", 0), e3)
    first = "total" not in places
    if not first:
        begin("total", sources[places["total"]], out)
    weight_imag = weights[member * local + pole, 0]
    weight_real = weights[member * local + pole, 1]

    columns = sb // extent
    finish("e0", "w1")
    mask_panel(w1, masks, 0, m1, m1t, sb, extent)
    couple(path, m1, x1, 1, form, sb)
    finish("w3", "w2", "e2", "e3")
    mask_panel(w2, masks, columns, m2, m2t, sb, extent)
    close(path, m1t, x1, e1, 1, form, sb)
    mask_panel(w3, masks, 3 * columns, m3, m3t, sb, extent)
    couple(path, m2, x2, 2, form, sb)
    close(path, m2t, x2, e2, 2, form, sb)
    if not first:
        finish("total")

    def add_rows(rows, value):
        if first:
            out[rows, :] = value
        else:
            out[rows, :] = out[rows, :] + value

    for low, high, product in tiled_dot(path, m3, slice(0, 3 * sb), 6 * sb, form):
        real, imag = product[:, 0:sb], product[:, sb : 2 * sb]
        add_rows(slice(low, high), -(weight_imag * imag + weight_real * real))
        inner = slice(low % sb, low % sb + high - low)
        pack_right(x3, low // sb, inner, real.astype(BF16), imag.astype(BF16), sb)
    for low, high, product in tiled_dot(m3t, x3, slice(0, sb), 6 * sb, form):
        real = product[:, 0:sb] + e3[0, low:high, :].astype(F32)
        imag = product[:, sb : 2 * sb] + e3[1, low:high, :].astype(F32)
        add_rows(slice(3 * sb + low, 3 * sb + high), weight_imag * imag + weight_real * real)


def run_pole(pole, local, per_leaf, form, masks, weights, pieces, total, sb, extent):
    sources, places = [], {}

    def operand(array):
        for index, known in enumerate(sources):
            if known is array:
                return index
        sources.append(array)
        return len(sources) - 1

    for name, turns in pieces.items():
        places[name] = {turn: (operand(piece[0]), *piece[1:]) for turn, piece in turns.items()}
    if total is not None:
        places["total"] = operand(total)
    operands = [masks, weights, *sources]
    smem = pl.BlockSpec(memory_space=pltpu.SMEM)
    anywhere = pl.BlockSpec(memory_space=pl.ANY)
    vmem = lambda *shape: pltpu.VMEM(shape, BF16)
    return pl.pallas_call(
        functools.partial(pole_kernel, pole, local, per_leaf, form, places, sb, extent),
        out_shape=jax.ShapeDtypeStruct((4 * sb, sb), F32),
        in_specs=[smem] * 2 + [anywhere] * len(sources),
        out_specs=pl.BlockSpec(memory_space=pltpu.VMEM),
        scratch_shapes=[
            vmem(3 * sb, 6 * sb),
            vmem(2, sb, sb),
            vmem(2, sb, sb),
            vmem(2, 2 * sb, sb),
            vmem(2, sb, sb),
            vmem(2, 3 * sb, sb),
            vmem(2, sb, sb),
            vmem(2 * sb, 2 * sb),
            vmem(sb, 2 * sb),
            vmem(4 * sb, 2 * sb),
            vmem(sb, 4 * sb),
            vmem(6 * sb, 2 * sb),
            vmem(sb, 6 * sb),
            vmem(2 * sb, 2 * sb),
            vmem(4 * sb, 2 * sb),
            vmem(6 * sb, 2 * sb),
            pltpu.SemaphoreType.DMA((32,)),
        ],
        compiler_params=pltpu.CompilerParams(vmem_limit_bytes=56 * 1024 * 1024),
        cost_estimate=pl.CostEstimate(
            flops=160 * sb**3, bytes_accessed=80 * sb * sb, transcendentals=0
        ),
        name="pole_" + str(pole),
    )(*operands)


def shards(
    root_band,
    w_one,
    e_one,
    w_two,
    e_two,
    w_three,
    e_three,
    mask_one,
    mask_two,
    mask_three,
    pole_weights,
):
    devices = lax.axis_size("wide")
    per_leaf = devices // 8
    device_index = lax.axis_index("wide")
    leaf = device_index // per_leaf
    member = device_index % per_leaf
    local = root_band.shape[0]
    sb = w_three.shape[-1]
    quarter, half = sb // 4, sb // 2

    def turn(block, bits, after=()):
        if after:
            block = lax.optimization_barrier((block, *after))[0]
        route = [(low, low ^ bits * per_leaf) for low in range(devices)]
        return lax.ppermute(block, "wide", route)

    def gather(block, count):
        groups = []
        for low in range(devices):
            if low // per_leaf // 2 % count == 0:
                groups.append([low + 2 * per_leaf * step for step in range(count)])
        return lax.all_gather(block, "wide", axis_index_groups=groups)

    early = (local + 1) // 2
    batches = [slice(0, early)] + ([slice(early, local)] if local > early else [])
    root_y = turn(root_band, 1)
    packs = [jnp.concatenate([w_one[batch], e_one[batch]], axis=2) for batch in batches]
    one_y = [turn(pack, 1) for pack in packs]
    root_y, *one_y = lax.optimization_barrier((root_y, *one_y))
    root_all = [gather(root_band, 4), gather(root_y, 4)]
    one_all = [[gather(pack, 2), gather(pack_y, 2)] for pack, pack_y in zip(packs, one_y)]
    panels = [jnp.concatenate([w_two[pole], e_two[pole]], axis=1) for pole in range(local - 1)]
    two_y = [turn(panel, 1) for panel in panels]
    last_two_y = turn(w_two[local - 1], 1)
    last_corner_y = turn(e_two[local - 1], 1)

    masks = jnp.concatenate(
        [
            lax.dynamic_index_in_dim(mask_one, leaf // 4, 0, keepdims=False),
            lax.dynamic_index_in_dim(mask_two, leaf // 2, 0, keepdims=False),
            lax.dynamic_index_in_dim(mask_three, leaf, 0, keepdims=False),
        ],
        axis=0,
    )
    density = None
    for pole in range(local):
        batch = 0 if pole < early else 1
        at = pole - batches[batch].start
        pieces = {"root": {}, "w_one": {}, "e_one": {}}
        for source in range(2):
            for level in range(4):
                pieces["root"][4 * source + level] = (root_all[source], (level, pole), None, None)
            for level in range(2):
                piece = (one_all[batch][source], (level, at))
                pieces["w_one"][2 * source + level] = (*piece, 0, quarter)
                pieces["e_one"][2 * source + level] = (*piece, quarter, 2 * quarter)
        pieces["w_two"] = {0: (w_two, pole, None, None)}
        pieces["e_two"] = {0: (e_two, pole, None, None)}
        if pole < local - 1:
            pieces["w_two"][1] = (two_y[pole], None, 0, sb)
            pieces["e_two"][1] = (two_y[pole], None, sb, sb + half)
        else:
            pieces["w_two"][1] = (last_two_y, None, None, None)
            pieces["e_two"][1] = (last_corner_y, None, None, None)
        pieces["w_three"] = {0: (w_three, pole, None, None)}
        pieces["e_three"] = {0: (e_three, pole, None, None)}
        density = run_pole(
            pole,
            local,
            per_leaf,
            FORMS[pole % len(FORMS)],
            masks,
            pole_weights,
            pieces,
            density,
            sb,
            sb // mask_one.shape[-1],
        )
    for level_bit in range(per_leaf.bit_length() - 2, -1, -1):
        half_count = density.shape[0] // 2
        lower_rows = density[:half_count]
        upper_rows = density[half_count:]
        bit_set = member // (1 << level_bit) % 2 == 1
        kept_rows = jnp.where(bit_set, upper_rows, lower_rows)
        sent_rows = jnp.where(bit_set, lower_rows, upper_rows)
        route = [(low, low ^ 1 << level_bit) for low in range(devices)]
        density = kept_rows + lax.ppermute(sent_rows, "wide", route)
    return density


def solution(mesh):
    split = P(("groups", "wide"), None, None, None)
    return jax.shard_map(
        shards,
        mesh=mesh,
        in_specs=(split,) * 7 + (P("groups", None, None),) * 3 + (P(),),
        out_specs=P(("groups", "wide"), None),
        check_vma=False,
    )
```

```python
import functools

import jax
import jax.numpy as jnp
from jax import lax
from jax.experimental import pallas as pl
from jax.experimental.pallas import tpu as pltpu
from jax.sharding import PartitionSpec as P

BF16 = jnp.bfloat16
F32 = jnp.float32
SMEM = pl.BlockSpec(memory_space=pltpu.SMEM)
ANYWHERE = pl.BlockSpec(memory_space=pl.ANY)
WHOLE = pl.BlockSpec(memory_space=pltpu.VMEM)


def mask_row(masks, tile, extent, width):
    lane = lax.broadcasted_iota(jnp.int32, (1, width), 1)
    row = jnp.zeros((1, width), F32)
    for column in range(width // extent):
        value = masks[tile, column].astype(F32)
        inside = (lane >= column * extent) & (lane < (column + 1) * extent)
        row = jnp.where(inside, value, row)
    return row.astype(BF16)


def pack_right(target, first, real, imag, sb):
    count = real.shape[0]
    low = 2 * sb * (first // sb) + first % sb
    target[low : low + count, 0:sb] = real
    target[low : low + count, sb : 2 * sb] = imag
    target[low + sb : low + sb + count, 0:sb] = -imag
    target[low + sb : low + sb + count, sb : 2 * sb] = real


def mask_panel(raw, masks, base, right, turned, sb):
    columns = masks.shape[1]
    extent = sb // columns
    for tile in range(raw.shape[1] // extent):
        row = mask_row(masks, base + tile, extent, sb)
        first = tile * extent
        real = raw[0, first : first + extent, :] * row
        imag = raw[1, first : first + extent, :] * row
        pack_right(right, first, real, imag, sb)
        low = 2 * sb * (first // sb) + first % sb
        turned[:, low : low + extent] = real.T
        turned[:, low + sb : low + sb + extent] = imag.T


def dot(left, right):
    return jnp.dot(left, right, preferred_element_type=F32)


def couple(path, right, packed, level, sb):
    size = 2 * sb * level
    for block in range(level):
        rows = slice(block * sb, (block + 1) * sb)
        product = dot(path[rows, 0:size], right[...]).astype(BF16)
        real, imag = product[:, 0:sb], product[:, sb : 2 * sb]
        path[rows, size : size + 2 * sb] = -product
        pack_right(packed, block * sb, real, imag, sb)
        low = 2 * sb * block
        path[level * sb : (level + 1) * sb, low : low + sb] = -real.T
        path[level * sb : (level + 1) * sb, low + sb : low + 2 * sb] = -imag.T


def close(path, product, corner, level, sb):
    rows = slice(level * sb, (level + 1) * sb)
    for part in range(2):
        own = product[:, part * sb : (part + 1) * sb] + corner[part].astype(F32)
        low = 2 * sb * level + part * sb
        path[rows, low : low + sb] = own.astype(BF16)


class Copies:
    def __init__(self, sems):
        self.sems = sems
        self.started = {}
        self.count = 0

    def start(self, name, source, target):
        copy = pltpu.make_async_copy(source, target, self.sems.at[self.count])
        self.count += 1
        copy.start()
        self.started.setdefault(name, []).append(copy)

    def wait(self, *names):
        for name in names:
            for copy in self.started.pop(name):
                copy.wait()


def rows_at(index, size):
    return pl.ds(pl.multiple_of(index * size, size), size)


def fetch_root(copies, find, leaf, path, sb):
    for turn in range(8):
        rows = rows_at(leaf ^ turn, sb // 8)
        source = find("root", turn)
        for part in range(2):
            copies.start("root", source.at[part], path.at[rows, part * sb : (part + 1) * sb])


def fetch_pieces(copies, find, leaf, name, turns, target):
    for turn in range(turns):
        size = target.shape[1] // turns
        rows = rows_at((leaf & (turns - 1)) ^ turn, size)
        copies.start(name, find(name, turn), target.at[:, rows, :])


def finder(sources, places):
    def find(name, turn=0):
        operand, index, low, high = places[name][turn]
        source = sources[operand]
        if index is not None:
            source = source.at[index]
        return source if low is None else source.at[:, low:high, :]

    return find


def coordinates(local, per_leaf, pole, weights):
    device = lax.axis_index("wide")
    leaf, member = device // per_leaf, device % per_leaf
    return leaf, weights[member * local + pole, 0], weights[member * local + pole, 1]


def add_rows(out, rows, value, running):
    if running:
        out[rows, :] = out[rows, :] + value
    else:
        out[rows, :] = value


def leaf_panel_kernel(sb, find_places, masks, w_three, right, turned, raw, sems):
    copies = Copies(sems)
    copies.start("w", w_three.at[find_places], raw)
    copies.wait("w")
    mask_panel(raw, masks, 3 * masks.shape[1], right, turned, sb)


def whole_kernel(sb, key, places, running, *refs):
    masks, weights = refs[:2]
    sources, rest = refs[2:-17], refs[-17:]
    upper, lower, path, w1, e1, w2, e2, m3, m3t, e3, m1, m1t, m2, m2t, x, x3, sems = rest
    leaf, weight_imag, weight_real = coordinates(*key, weights)
    find = finder(sources, places)
    copies = Copies(sems)
    columns = masks.shape[1]
    fetch_root(copies, find, leaf, path, sb)
    fetch_pieces(copies, find, leaf, "w_one", 4, w1)
    fetch_pieces(copies, find, leaf, "e_one", 4, e1)
    fetch_pieces(copies, find, leaf, "w_two", 2, w2)
    fetch_pieces(copies, find, leaf, "e_two", 2, e2)
    copies.start("m3", find("m_three"), m3)
    copies.start("m3", find("turned_three"), m3t)
    copies.start("m3", find("e_three"), e3)
    if running:
        copies.start("total", find("upper"), upper)
        copies.start("total", find("lower"), lower)
    copies.wait("root", "w_one", "e_one")
    mask_panel(w1, masks, 0, m1, m1t, sb)
    couple(path, m1, x, 1, sb)
    copies.wait("w_two", "e_two", "m3")
    if running:
        copies.wait("total")
    mask_panel(w2, masks, columns, m2, m2t, sb)
    close(path, dot(m1t[...], x[0 : 2 * sb, :]), e1, 1, sb)
    couple(path, m2, x, 2, sb)
    close(path, dot(m2t[...], x[...]), e2, 2, sb)
    for block in range(3):
        rows = slice(block * sb, (block + 1) * sb)
        product = dot(path[rows, :], m3[...])
        real, imag = product[:, 0:sb], product[:, sb : 2 * sb]
        value = -(weight_imag * imag + weight_real * real)
        if block < 2:
            add_rows(upper, rows, value, running)
        else:
            add_rows(lower, slice(0, sb), value, running)
        pack_right(x3, block * sb, real.astype(BF16), imag.astype(BF16), sb)
    product = dot(m3t[...], x3[...])
    real = product[:, 0:sb] + e3[0].astype(F32)
    imag = product[:, sb : 2 * sb] + e3[1].astype(F32)
    add_rows(lower, slice(sb, 2 * sb), weight_imag * imag + weight_real * real, running)


def first_kernel(sb, key, places, *refs):
    masks, weights = refs[:2]
    sources, rest = refs[2:-9], refs[-9:]
    path, share, w1, e1, m3, m1, m1t, x, sems = rest
    leaf, _, _ = coordinates(*key, weights)
    find = finder(sources, places)
    copies = Copies(sems)
    fetch_root(copies, find, leaf, path, sb)
    fetch_pieces(copies, find, leaf, "w_one", 4, w1)
    fetch_pieces(copies, find, leaf, "e_one", 4, e1)
    copies.start("m3", find("m_three").at[0 : 4 * sb, :], m3)
    copies.wait("root", "w_one", "e_one")
    mask_panel(w1, masks, 0, m1, m1t, sb)
    couple(path, m1, x, 1, sb)
    close(path, dot(m1t[...], x[...]), e1, 1, sb)
    copies.wait("m3")
    for block in range(2):
        rows = slice(block * sb, (block + 1) * sb)
        share[rows, :] = dot(path[rows, :], m3[...])


def second_kernel(sb, key, places, running, *refs):
    masks, weights = refs[:2]
    sources, rest = refs[2:-15], refs[-15:]
    upper, corner, low_share, leaf_share, path, share, w2, m3, m3t, e3, m2, m2t, x, x3, sems = rest
    leaf, weight_imag, weight_real = coordinates(*key, weights)
    find = finder(sources, places)
    copies = Copies(sems)
    columns = masks.shape[1]
    fetch_pieces(copies, find, leaf, "w_two", 2, w2)
    copies.start("path", find("path"), path.at[0 : 2 * sb, 0 : 4 * sb])
    copies.start("m3", find("m_three"), m3)
    copies.start("m3", find("share"), share)
    copies.start("m3", find("turned_three").at[:, 0 : 4 * sb], m3t)
    copies.start("m3", find("e_three"), e3)
    if running:
        copies.start("m3", find("upper"), upper)
    copies.wait("w_two")
    mask_panel(w2, masks, columns, m2, m2t, sb)
    copies.wait("path")
    couple(path, m2, x, 2, sb)
    copies.wait("m3")
    for block in range(2):
        rows = slice(block * sb, (block + 1) * sb)
        product = share[rows, :] + dot(path[rows, 4 * sb :], m3[4 * sb :, :])
        real, imag = product[:, 0:sb], product[:, sb : 2 * sb]
        add_rows(upper, rows, -(weight_imag * imag + weight_real * real), running)
        pack_right(x3, block * sb, real.astype(BF16), imag.astype(BF16), sb)
    corner[...] = dot(m2t[...], x[...])
    low_share[...] = dot(path[2 * sb :, 0 : 4 * sb], m3[0 : 4 * sb, :])
    product = dot(m3t[...], x3[...])
    for part in range(2):
        where = slice(part * sb, (part + 1) * sb)
        leaf_share[:, where] = product[:, where] + e3[part].astype(F32)


def third_kernel(sb, key, places, running, *refs):
    weights = refs[0]
    sources, rest = refs[1:-10], refs[-10:]
    lower, e2, corner, low_share, leaf_share, m3, m3t, left, x3, sems = rest
    leaf, weight_imag, weight_real = coordinates(*key, weights)
    find = finder(sources, places)
    copies = Copies(sems)
    fetch_pieces(copies, find, leaf, "e_two", 2, e2)
    copies.start("corner", find("corner"), corner)
    copies.start("m3", find("m_three").at[4 * sb :, :], m3)
    copies.start("m3", find("low_share"), low_share)
    copies.start("last", find("turned_three").at[:, 4 * sb :], m3t)
    copies.start("last", find("leaf_share"), leaf_share)
    if running:
        copies.start("m3", find("lower"), lower)
    copies.wait("e_two", "corner")
    for part in range(2):
        where = slice(part * sb, (part + 1) * sb)
        left[:, where] = (corner[:, where] + e2[part].astype(F32)).astype(BF16)
    copies.wait("m3")
    product = low_share[...] + dot(left[...], m3[...])
    real, imag = product[:, 0:sb], product[:, sb : 2 * sb]
    add_rows(lower, slice(0, sb), -(weight_imag * imag + weight_real * real), running)
    pack_right(x3, 0, real.astype(BF16), imag.astype(BF16), sb)
    copies.wait("last")
    product = leaf_share[...] + dot(m3t[...], x3[...])
    real, imag = product[:, 0:sb], product[:, sb : 2 * sb]
    add_rows(lower, slice(sb, 2 * sb), weight_imag * imag + weight_real * real, running)


def call(kernel, name, scalars, pieces, outs, scratch, flops):
    sources, places = [], {}

    def operand(array):
        for index, known in enumerate(sources):
            if known is array:
                return index
        sources.append(array)
        return len(sources) - 1

    for key, turns in pieces.items():
        places[key] = {turn: (operand(piece[0]), *piece[1:]) for turn, piece in turns.items()}
    results = [jax.ShapeDtypeStruct(shape, kind) for shape, kind in outs]
    return pl.pallas_call(
        kernel(places),
        out_shape=results,
        in_specs=[SMEM] * len(scalars) + [ANYWHERE] * len(sources),
        out_specs=[WHOLE] * len(results),
        scratch_shapes=[pltpu.VMEM(shape, kind) for shape, kind in scratch]
        + [pltpu.SemaphoreType.DMA((36,))],
        compiler_params=pltpu.CompilerParams(vmem_limit_bytes=60 << 20),
        cost_estimate=pl.CostEstimate(flops=flops, bytes_accessed=1 << 20, transcendentals=0),
        name=name,
    )(*scalars, *sources)


def shards(
    root_band,
    w_one,
    e_one,
    w_two,
    e_two,
    w_three,
    e_three,
    mask_one,
    mask_two,
    mask_three,
    pole_weights,
):
    devices = lax.axis_size("wide")
    per_leaf = devices // 8
    device_index = lax.axis_index("wide")
    leaf = device_index // per_leaf
    member = device_index % per_leaf
    local = root_band.shape[0]
    sb = w_three.shape[-1]
    quarter, half = sb // 4, sb // 2
    last = local - 1

    def turn(block, bits, *after):
        after = [array for array in after if array is not None]
        if after:
            block = lax.optimization_barrier((block, *after))[0]
        route = [(low, low ^ bits * per_leaf) for low in range(devices)]
        return lax.ppermute(block, "wide", route)

    early = (local + 1) // 2
    batches = [slice(0, early)] + ([slice(early, local)] if local > early else [])
    late = len(batches) > 1
    packs = [jnp.concatenate([w_one[batch], e_one[batch]], axis=2) for batch in batches]
    panels = [jnp.concatenate([w_two[pole], e_two[pole]], axis=1) for pole in range(last)]

    root = {0: root_band, 1: turn(root_band, 1)}
    one = [{1: turn(packs[0], 1)}]
    for bits in (2, 4, 6):
        root[bits] = turn(root_band, bits)
    two = []
    if last > 0:
        two.append(turn(panels[0], 1, root[1]))
    one[0][2] = turn(packs[0], 2, root[2])
    root[3] = turn(root[1], 2, root[4])
    if late:
        one.append({1: turn(packs[1], 1, one[0][1])})
    root[5] = turn(root[1], 4, root[6])
    root[7] = turn(root[1], 6, one[0][2])
    if last > 1:
        two.append(turn(panels[1], 1, two[0]))
    one[0][3] = turn(one[0][1], 2, root[3])
    if late:
        one[1][2] = turn(packs[1], 2, root[5])
    if last > 2:
        two.append(turn(panels[2], 1, one[1][1]))
    if late:
        one[1][3] = turn(one[1][1], 2, root[7])
    last_two = turn(w_two[last], 1, one[0][3])
    last_corner = turn(e_two[last], 1, two[1] if last > 1 else None)

    masks = jnp.concatenate(
        [
            lax.dynamic_index_in_dim(mask_one, leaf // 4, 0, keepdims=False),
            lax.dynamic_index_in_dim(mask_two, leaf // 2, 0, keepdims=False),
            lax.dynamic_index_in_dim(mask_three, leaf, 0, keepdims=False),
        ],
        axis=0,
    )
    upper = lower = None
    gated_masks = masks
    single = lambda array, index=None: {0: (array, index, None, None)}
    unit = 2 * sb**3
    for pole in range(local):
        m_three, turned_three = call(
            lambda places, pole=pole: functools.partial(leaf_panel_kernel, sb, pole),
            "leaf_panel_" + str(pole),
            [masks],
            {"w_three": single(w_three)},
            [((6 * sb, 2 * sb), BF16), ((sb, 6 * sb), BF16)],
            [((2, 3 * sb, sb), BF16)],
            8 * unit,
        )
        batch = 0 if pole < early else 1
        at = pole - batches[batch].start
        pieces = {"root": {bits: (root[bits], pole, None, None) for bits in range(8)}}
        pieces["w_one"], pieces["e_one"] = single(w_one, pole), single(e_one, pole)
        for bits in (1, 2, 3):
            pieces["w_one"][bits] = (one[batch][bits], at, 0, quarter)
            pieces["e_one"][bits] = (one[batch][bits], at, quarter, 2 * quarter)
        pieces["m_three"] = single(m_three)
        key = (local, per_leaf, pole)
        running = upper is not None
        if pole == last - 1 and running:
            gated_masks = lax.optimization_barrier((masks, upper))[0]
        if pole < last:
            pieces["w_two"] = {**single(w_two, pole), 1: (two[pole], None, 0, sb)}
            pieces["e_two"] = {**single(e_two, pole), 1: (two[pole], None, sb, sb + half)}
            pieces["turned_three"] = single(turned_three)
            pieces["e_three"] = single(e_three, pole)
            if running:
                pieces["upper"], pieces["lower"] = single(upper), single(lower)
            upper, lower = call(
                lambda places: functools.partial(whole_kernel, sb, key, places, running),
                "pole_" + str(pole),
                [masks, pole_weights],
                pieces,
                [((2 * sb, sb), F32), ((2 * sb, sb), F32)],
                [
                    ((3 * sb, 6 * sb), BF16),
                    ((2, sb, sb), BF16),
                    ((2, sb, sb), BF16),
                    ((2, 2 * sb, sb), BF16),
                    ((2, sb, sb), BF16),
                    ((6 * sb, 2 * sb), BF16),
                    ((sb, 6 * sb), BF16),
                    ((2, sb, sb), BF16),
                    ((2 * sb, 2 * sb), BF16),
                    ((sb, 2 * sb), BF16),
                    ((4 * sb, 2 * sb), BF16),
                    ((sb, 4 * sb), BF16),
                    ((4 * sb, 2 * sb), BF16),
                    ((6 * sb, 2 * sb), BF16),
                ],
                80 * unit,
                )
            continue
        path, share = call(
            lambda places: functools.partial(first_kernel, sb, key, places),
            "pole_first",
            [gated_masks, pole_weights],
            pieces,
            [((2 * sb, 4 * sb), BF16), ((2 * sb, 2 * sb), F32)],
            [
                ((2, sb, sb), BF16),
                ((2, sb, sb), BF16),
                ((4 * sb, 2 * sb), BF16),
                ((2 * sb, 2 * sb), BF16),
                ((sb, 2 * sb), BF16),
                ((2 * sb, 2 * sb), BF16),
            ],
            24 * unit,
        )
        pieces = {
            "w_two": {**single(w_two, pole), 1: (last_two, None, None, None)},
            "path": single(path),
            "m_three": single(m_three),
            "share": single(share),
            "turned_three": single(turned_three),
            "e_three": single(e_three, pole),
        }
        if running:
            pieces["upper"] = single(upper)
        upper, corner, low_share, leaf_share = call(
            lambda places: functools.partial(second_kernel, sb, key, places, running),
            "pole_second",
            [masks, pole_weights],
            pieces,
            [((2 * sb, sb), F32)] + [((sb, 2 * sb), F32)] * 3,
            [
                ((3 * sb, 6 * sb), BF16),
                ((2 * sb, 2 * sb), F32),
                ((2, 2 * sb, sb), BF16),
                ((6 * sb, 2 * sb), BF16),
                ((sb, 4 * sb), BF16),
                ((2, sb, sb), BF16),
                ((4 * sb, 2 * sb), BF16),
                ((sb, 4 * sb), BF16),
                ((4 * sb, 2 * sb), BF16),
                ((4 * sb, 2 * sb), BF16),
            ],
            48 * unit,
        )
        pieces = {
            "e_two": {**single(e_two, pole), 1: (last_corner, None, None, None)},
            "corner": single(corner),
            "m_three": single(m_three),
            "low_share": single(low_share),
            "turned_three": single(turned_three),
            "leaf_share": single(leaf_share),
        }
        if running:
            pieces["lower"] = single(lower)
        (lower,) = call(
            lambda places: functools.partial(third_kernel, sb, key, places, running),
            "pole_third",
            [pole_weights],
            pieces,
            [((2 * sb, sb), F32)],
            [
                ((2, sb, sb), BF16),
                ((sb, 2 * sb), F32),
                ((sb, 2 * sb), F32),
                ((sb, 2 * sb), F32),
                ((2 * sb, 2 * sb), BF16),
                ((sb, 2 * sb), BF16),
                ((sb, 2 * sb), BF16),
                ((2 * sb, 2 * sb), BF16),
            ],
            8 * unit,
        )

    if per_leaf == 1:
        return jnp.concatenate([upper, lower], axis=0)
    bit = per_leaf // 2
    low_members = [low for low in range(devices) if low & bit == 0]
    upper = upper + lax.ppermute(upper, "wide", [(low | bit, low) for low in low_members])
    lower = lower + lax.ppermute(lower, "wide", [(low, low | bit) for low in low_members])
    density = jnp.where(member & bit == 0, upper, lower)
    while bit > 1:
        bit //= 2
        half_count = density.shape[0] // 2
        bit_set = member & bit != 0
        kept = jnp.where(bit_set, density[half_count:], density[:half_count])
        sent = jnp.where(bit_set, density[:half_count], density[half_count:])
        density = kept + lax.ppermute(sent, "wide", [(low, low ^ bit) for low in range(devices)])
    return density


def solution(mesh):
    split = P(("groups", "wide"), None, None, None)
    return jax.shard_map(
        shards,
        mesh=mesh,
        in_specs=(split,) * 7 + (P("groups", None, None),) * 3 + (P(),),
        out_specs=P(("groups", "wide"), None),
        check_vma=False,
    )
```

```python
import functools

import jax
import jax.numpy as jnp
from jax import lax
from jax.experimental import pallas as pl
from jax.experimental.pallas import tpu as pltpu
from jax.sharding import PartitionSpec as P

BF16 = jnp.bfloat16
F32 = jnp.float32
SMEM = pl.BlockSpec(memory_space=pltpu.SMEM)
ANYWHERE = pl.BlockSpec(memory_space=pl.ANY)


def mask_row(masks, tile, extent, width):
    lane = lax.broadcasted_iota(jnp.int32, (1, width), 1)
    row = jnp.zeros((1, width), F32)
    for column in range(width // extent):
        value = masks[tile, column].astype(F32)
        inside = (lane >= column * extent) & (lane < (column + 1) * extent)
        row = jnp.where(inside, value, row)
    return row.astype(BF16)


def pack_right(target, first, real, imag, sb):
    count = real.shape[0]
    low = 2 * sb * (first // sb) + first % sb
    target[low : low + count, 0:sb] = real
    target[low : low + count, sb : 2 * sb] = imag
    target[low + sb : low + sb + count, 0:sb] = -imag
    target[low + sb : low + sb + count, sb : 2 * sb] = real


def mask_panel(raw, masks, base, right, turned, sb):
    columns = masks.shape[1]
    extent = sb // columns
    for tile in range(raw.shape[1] // extent):
        row = mask_row(masks, base + tile, extent, sb)
        first = tile * extent
        real = raw[0, first : first + extent, :] * row
        imag = raw[1, first : first + extent, :] * row
        pack_right(right, first, real, imag, sb)
        low = 2 * sb * (first // sb) + first % sb
        turned[:, low : low + extent] = real.T
        turned[:, low + sb : low + sb + extent] = imag.T


def dot(left, right):
    return jnp.dot(left, right, preferred_element_type=F32)


def couple(path, right, packed, level, sb):
    size = 2 * sb * level
    for block in range(level):
        rows = slice(block * sb, (block + 1) * sb)
        product = dot(path[rows, 0:size], right[...]).astype(BF16)
        real, imag = product[:, 0:sb], product[:, sb : 2 * sb]
        path[rows, size : size + 2 * sb] = -product
        pack_right(packed, block * sb, real, imag, sb)
        low = 2 * sb * block
        path[level * sb : (level + 1) * sb, low : low + sb] = -real.T
        path[level * sb : (level + 1) * sb, low + sb : low + 2 * sb] = -imag.T


def close(path, product, corner, level, sb):
    rows = slice(level * sb, (level + 1) * sb)
    for part in range(2):
        own = product[:, part * sb : (part + 1) * sb] + corner[part].astype(F32)
        low = 2 * sb * level + part * sb
        path[rows, low : low + sb] = own.astype(BF16)


class Copies:
    def __init__(self, sems):
        self.sems = sems
        self.started = {}
        self.count = 0

    def start(self, name, source, target):
        copy = pltpu.make_async_copy(source, target, self.sems.at[self.count])
        self.count += 1
        copy.start()
        self.started.setdefault(name, []).append(copy)

    def wait(self, *names):
        for name in names:
            for copy in self.started.pop(name):
                copy.wait()


def rows_at(index, size):
    return pl.ds(pl.multiple_of(index * size, size), size)


def fetch_root(copies, find, leaf, path, sb):
    for turn in range(8):
        rows = rows_at(leaf ^ turn, sb // 8)
        source = find("root", turn)
        for part in range(2):
            copies.start("root", source.at[part], path.at[rows, part * sb : (part + 1) * sb])


def fetch_pieces(copies, find, leaf, name, turns, target):
    for turn in range(turns):
        size = target.shape[1] // turns
        rows = rows_at((leaf & (turns - 1)) ^ turn, size)
        copies.start(name, find(name, turn), target.at[:, rows, :])


def finder(sources, places):
    def find(name, turn=0):
        operand, index, low, high = places[name][turn]
        source = sources[operand]
        if index is not None:
            source = source.at[index]
        return source if low is None else source.at[:, low:high, :]

    return find


def coordinates(local, per_leaf, pole, weights):
    device = lax.axis_index("wide")
    leaf, member = device // per_leaf, device % per_leaf
    return leaf, weights[member * local + pole, 0], weights[member * local + pole, 1]


def add_rows(out, rows, value, running):
    if running:
        out[rows, :] = out[rows, :] + value
    else:
        out[rows, :] = value


def whole_kernel(sb, key, places, running, *refs):
    masks, weights = refs[:2]
    sources, rest = refs[2:-20], refs[-20:]
    upper_out, lower_out, upper, lower, path, w1, e1, w2, e2, w3, e3, m1, m1t, m2, m2t, m3, m3t, x, x3, sems = rest
    leaf, weight_imag, weight_real = coordinates(*key, weights)
    copies = Copies(sems)
    columns = masks.shape[1]
    find = finder(sources, places)
    fetch_root(copies, find, leaf, path, sb)
    fetch_pieces(copies, find, leaf, "w_one", 4, w1)
    fetch_pieces(copies, find, leaf, "e_one", 4, e1)
    fetch_pieces(copies, find, leaf, "w_two", 2, w2)
    copies.start("w_three", find("w_three"), w3)
    fetch_pieces(copies, find, leaf, "e_two", 2, e2)
    if running:
        copies.start("upper", find("upper"), upper)
        copies.start("lower", find("lower"), lower)
    copies.start("e_three", find("e_three"), e3)
    copies.wait("root", "w_one")
    mask_panel(w1, masks, 0, m1, m1t, sb)
    couple(path, m1, x, 1, sb)
    copies.wait("e_one", "w_two")
    mask_panel(w2, masks, columns, m2, m2t, sb)
    close(path, dot(m1t[...], x[0 : 2 * sb, :]), e1, 1, sb)
    couple(path, m2, x, 2, sb)
    copies.wait("w_three", "e_two")
    mask_panel(w3, masks, 3 * columns, m3, m3t, sb)
    close(path, dot(m2t[...], x[...]), e2, 2, sb)
    if running:
        copies.wait("upper")
    for block in range(2):
        rows = slice(block * sb, (block + 1) * sb)
        product = dot(path[rows, :], m3[...])
        real, imag = product[:, 0:sb], product[:, sb : 2 * sb]
        add_rows(upper, rows, -(weight_imag * imag + weight_real * real), running)
        pack_right(x3, block * sb, real.astype(BF16), imag.astype(BF16), sb)
    copies.start("out", upper, upper_out)
    if running:
        copies.wait("lower")
    product = dot(path[2 * sb :, :], m3[...])
    real, imag = product[:, 0:sb], product[:, sb : 2 * sb]
    add_rows(lower, slice(0, sb), -(weight_imag * imag + weight_real * real), running)
    pack_right(x3, 2 * sb, real.astype(BF16), imag.astype(BF16), sb)
    copies.start("out", lower.at[0:sb, :], lower_out.at[0:sb, :])
    copies.wait("e_three")
    product = dot(m3t[...], x3[...])
    real = product[:, 0:sb] + e3[0].astype(F32)
    imag = product[:, sb : 2 * sb] + e3[1].astype(F32)
    add_rows(lower, slice(sb, 2 * sb), weight_imag * imag + weight_real * real, running)
    copies.start("out", lower.at[sb:, :], lower_out.at[sb:, :])
    copies.wait("out")


def most_kernel(sb, key, places, running, *refs):
    masks, weights = refs[:2]
    sources, rest = refs[2:-25], refs[-25:]
    upper_out, corner_out, low_out, leaf_out, m3_low, m3t_low = rest[:6]
    upper, corner, low_share, leaf_share, path, w1, e1, w2, w3, e3, m1, m1t, m2, m2t, m3, m3t, x, x3, sems = rest[6:]
    leaf, weight_imag, weight_real = coordinates(*key, weights)
    copies = Copies(sems)
    columns = masks.shape[1]
    find = finder(sources, places)
    fetch_root(copies, find, leaf, path, sb)
    fetch_pieces(copies, find, leaf, "w_one", 4, w1)
    fetch_pieces(copies, find, leaf, "e_one", 4, e1)
    fetch_pieces(copies, find, leaf, "w_two", 2, w2)
    copies.start("w_three", find("w_three"), w3)
    if running:
        copies.start("upper", find("upper"), upper)
    copies.start("e_three", find("e_three"), e3)
    copies.wait("root", "w_one")
    mask_panel(w1, masks, 0, m1, m1t, sb)
    couple(path, m1, x, 1, sb)
    copies.wait("e_one", "w_two")
    mask_panel(w2, masks, columns, m2, m2t, sb)
    close(path, dot(m1t[...], x[0 : 2 * sb, :]), e1, 1, sb)
    couple(path, m2, x, 2, sb)
    copies.wait("w_three")
    mask_panel(w3, masks, 3 * columns, m3, m3t, sb)
    copies.start("out", m3.at[4 * sb :, :], m3_low)
    copies.start("out", m3t.at[:, 4 * sb :], m3t_low)
    corner[...] = dot(m2t[...], x[...])
    copies.start("out", corner, corner_out)
    if running:
        copies.wait("upper")
    for block in range(2):
        rows = slice(block * sb, (block + 1) * sb)
        product = dot(path[rows, :], m3[...])
        real, imag = product[:, 0:sb], product[:, sb : 2 * sb]
        add_rows(upper, rows, -(weight_imag * imag + weight_real * real), running)
        pack_right(x3, block * sb, real.astype(BF16), imag.astype(BF16), sb)
    copies.start("out", upper, upper_out)
    low_share[...] = dot(path[2 * sb :, 0 : 4 * sb], m3[0 : 4 * sb, :])
    copies.start("out", low_share, low_out)
    copies.wait("e_three")
    product = dot(m3t[:, 0 : 4 * sb], x3[...])
    for part in range(2):
        where = slice(part * sb, (part + 1) * sb)
        leaf_share[:, where] = product[:, where] + e3[part].astype(F32)
    copies.start("out", leaf_share, leaf_out)
    copies.wait("out")


def corner_kernel(sb, key, places, *refs):
    weights = refs[0]
    sources, rest = refs[1:-11], refs[-11:]
    lower_out, lower, e2, corner, low_share, leaf_share, m3_low, m3t_low, left, x3, sems = rest
    leaf, weight_imag, weight_real = coordinates(*key, weights)
    copies = Copies(sems)
    find = finder(sources, places)
    fetch_pieces(copies, find, leaf, "e_two", 2, e2)
    copies.start("corner", find("corner"), corner)
    copies.start("low", find("m3_low"), m3_low)
    copies.start("low", find("low_share"), low_share)
    copies.start("leaf", find("m3t_low"), m3t_low)
    copies.start("leaf", find("leaf_share"), leaf_share)
    copies.wait("e_two", "corner")
    for part in range(2):
        where = slice(part * sb, (part + 1) * sb)
        left[:, where] = (corner[:, where] + e2[part].astype(F32)).astype(BF16)
    copies.wait("low")
    product = low_share[...] + dot(left[...], m3_low[...])
    real, imag = product[:, 0:sb], product[:, sb : 2 * sb]
    lower[0:sb, :] = -(weight_imag * imag + weight_real * real)
    pack_right(x3, 0, real.astype(BF16), imag.astype(BF16), sb)
    copies.start("out", lower.at[0:sb, :], lower_out.at[0:sb, :])
    copies.wait("leaf")
    product = leaf_share[...] + dot(m3t_low[...], x3[...])
    real, imag = product[:, 0:sb], product[:, sb : 2 * sb]
    lower[sb : 2 * sb, :] = weight_imag * imag + weight_real * real
    copies.start("out", lower.at[sb:, :], lower_out.at[sb:, :])
    copies.wait("out")


def call(kernel, name, scalars, pieces, outs, scratch, flops):
    sources, places = [], {}

    def operand(array):
        for index, known in enumerate(sources):
            if known is array:
                return index
        sources.append(array)
        return len(sources) - 1

    for key, turns in pieces.items():
        places[key] = {turn: (operand(piece[0]), *piece[1:]) for turn, piece in turns.items()}
    results = [jax.ShapeDtypeStruct(shape, kind) for shape, kind, _ in outs]
    return pl.pallas_call(
        kernel(places),
        out_shape=results,
        in_specs=[SMEM] * len(scalars) + [ANYWHERE] * len(sources),
        out_specs=[spec for _, _, spec in outs],
        scratch_shapes=[pltpu.VMEM(shape, kind) for shape, kind in scratch]
        + [pltpu.SemaphoreType.DMA((40,))],
        compiler_params=pltpu.CompilerParams(vmem_limit_bytes=60 << 20),
        cost_estimate=pl.CostEstimate(flops=flops, bytes_accessed=1 << 20, transcendentals=0),
        name=name,
    )(*scalars, *sources)


def shards(
    root_band,
    w_one,
    e_one,
    w_two,
    e_two,
    w_three,
    e_three,
    mask_one,
    mask_two,
    mask_three,
    pole_weights,
):
    devices = lax.axis_size("wide")
    per_leaf = devices // 8
    device_index = lax.axis_index("wide")
    leaf = device_index // per_leaf
    member = device_index % per_leaf
    local = root_band.shape[0]
    sb = w_three.shape[-1]
    quarter, half = sb // 4, sb // 2
    last = local - 1

    def turn(block, bits, *after):
        after = [array for array in after if array is not None]
        if after:
            block = lax.optimization_barrier((block, *after))[0]
        route = [(low, low ^ bits * per_leaf) for low in range(devices)]
        return lax.ppermute(block, "wide", route)

    early = (local + 1) // 2
    batches = [slice(0, early)] + ([slice(early, local)] if local > early else [])
    late = len(batches) > 1
    packs = [jnp.concatenate([w_one[batch], e_one[batch]], axis=2) for batch in batches]
    panels = [jnp.concatenate([w_two[pole], e_two[pole]], axis=1) for pole in range(last)]

    root = {0: root_band, 1: turn(root_band, 1)}
    root[2], root[6] = turn(root_band, 2), turn(root_band, 6)
    one = [{1: turn(packs[0], 1), 2: turn(packs[0], 2)}]
    two = []
    if last > 0:
        two.append(turn(panels[0], 1, root[1]))
    root[4] = turn(root_band, 4, root[2])
    root[7] = turn(root[1], 6, root[6])
    root[5] = turn(root[1], 4, one[0][2])
    root[3] = turn(root[1], 2, root[4])
    if late:
        one.append({1: turn(packs[1], 1, one[0][1])})
    one[0][3] = turn(one[0][1], 2, root[7])
    if last > 1:
        two.append(turn(panels[1], 1, two[0]))
    if late:
        one[1][2] = turn(packs[1], 2, root[5])
        one[1][3] = turn(one[1][1], 2, root[3])
    if last > 2:
        two.append(turn(panels[2], 1, one[1][1]))
    last_two = turn(w_two[last], 1, one[0][3], *two[1:2])
    last_corner = turn(e_two[last], 1, *two[2:3])

    masks = jnp.concatenate(
        [
            lax.dynamic_index_in_dim(mask_one, leaf // 4, 0, keepdims=False),
            lax.dynamic_index_in_dim(mask_two, leaf // 2, 0, keepdims=False),
            lax.dynamic_index_in_dim(mask_three, leaf, 0, keepdims=False),
        ],
        axis=0,
    )
    upper = lower = None
    single = lambda array, index=None: {0: (array, index, None, None)}
    unit = 2 * sb**3
    for pole in range(local):
        batch = 0 if pole < early else 1
        at = pole - batches[batch].start
        pieces = {"root": {bits: (root[bits], pole, None, None) for bits in range(8)}}
        pieces["w_one"], pieces["e_one"] = single(w_one, pole), single(e_one, pole)
        for bits in (1, 2, 3):
            pieces["w_one"][bits] = (one[batch][bits], at, 0, quarter)
            pieces["e_one"][bits] = (one[batch][bits], at, quarter, 2 * quarter)
        pieces["w_three"], pieces["e_three"] = single(w_three, pole), single(e_three, pole)
        key = (local, per_leaf, pole)
        running = upper is not None
        if running:
            pieces["upper"] = single(upper)
        halves = [((2 * sb, sb), F32)]
        shares = [((sb, 2 * sb), F32)] * 3
        raw = [((2, sb, sb), BF16)]
        packed = [
            ((2 * sb, 2 * sb), BF16),
            ((sb, 2 * sb), BF16),
            ((4 * sb, 2 * sb), BF16),
            ((sb, 4 * sb), BF16),
            ((6 * sb, 2 * sb), BF16),
            ((sb, 6 * sb), BF16),
            ((4 * sb, 2 * sb), BF16),
        ]
        path = [((3 * sb, 6 * sb), BF16)]
        two_raw, three_raw = [((2, 2 * sb, sb), BF16)], [((2, 3 * sb, sb), BF16)]
        if pole < last:
            pieces["w_two"] = {**single(w_two, pole), 1: (two[pole], None, 0, sb)}
            pieces["e_two"] = {**single(e_two, pole), 1: (two[pole], None, sb, sb + half)}
            if running:
                pieces["lower"] = single(lower)
            upper, lower = call(
                lambda places: functools.partial(whole_kernel, sb, key, places, running),
                "pole_" + str(pole),
                [masks, pole_weights],
                pieces,
                [((2 * sb, sb), F32, ANYWHERE), ((2 * sb, sb), F32, ANYWHERE)],
                halves * 2 + path + raw * 2 + two_raw + raw + three_raw + raw + packed
                + [((6 * sb, 2 * sb), BF16)],
                80 * unit,
                )
            continue
        pieces["w_two"] = {**single(w_two, pole), 1: (last_two, None, None, None)}
        upper, *between = call(
            lambda places: functools.partial(most_kernel, sb, key, places, running),
            "pole_most",
            [masks, pole_weights],
            pieces,
            [((2 * sb, sb), F32, ANYWHERE)]
            + [((sb, 2 * sb), F32, ANYWHERE)] * 3
            + [((2 * sb, 2 * sb), BF16, ANYWHERE), ((sb, 2 * sb), BF16, ANYWHERE)],
            halves + shares + path + raw * 2 + two_raw + three_raw + raw + packed
            + [((4 * sb, 2 * sb), BF16)],
            72 * unit,
        )
        names = ("corner", "low_share", "leaf_share", "m3_low", "m3t_low")
        pieces = {name: single(array) for name, array in zip(names, between)}
        pieces["e_two"] = {**single(e_two, pole), 1: (last_corner, None, None, None)}
        (corner_rows,) = call(
            lambda places: functools.partial(corner_kernel, sb, key, places),
            "pole_corner",
            [pole_weights],
            pieces,
            [((2 * sb, sb), F32, ANYWHERE)],
            halves + raw + shares
            + [((2 * sb, 2 * sb), BF16)] + [((sb, 2 * sb), BF16)] * 2 + [((2 * sb, 2 * sb), BF16)],
            8 * unit,
        )

    if per_leaf == 1:
        if lower is not None:
            corner_rows = lower + corner_rows
        return jnp.concatenate([upper, corner_rows], axis=0)
    bit = per_leaf // 2
    low_members = [low for low in range(devices) if low & bit == 0]
    to_low = [(low | bit, low) for low in low_members]
    to_high = [(low, low | bit) for low in low_members]
    is_low = member & bit == 0
    upper = upper + lax.ppermute(upper, "wide", to_low)
    if lower is None:
        early_rows = jnp.where(is_low, upper, 0.0)
    else:
        early_rows = jnp.where(is_low, upper, lower + lax.ppermute(lower, "wide", to_high))
    early_rows = lax.optimization_barrier(early_rows)
    late_rows = corner_rows + lax.ppermute(corner_rows, "wide", to_high)
    density = early_rows + jnp.where(is_low, 0.0, late_rows)
    while bit > 1:
        bit //= 2
        half_count = density.shape[0] // 2
        bit_set = member & bit != 0
        kept = jnp.where(bit_set, density[half_count:], density[:half_count])
        sent = jnp.where(bit_set, density[:half_count], density[half_count:])
        density = kept + lax.ppermute(sent, "wide", [(low, low ^ bit) for low in range(devices)])
    return density


def solution(mesh):
    split = P(("groups", "wide"), None, None, None)
    return jax.shard_map(
        shards,
        mesh=mesh,
        in_specs=(split,) * 7 + (P("groups", None, None),) * 3 + (P(),),
        out_specs=P(("groups", "wide"), None),
        check_vma=False,
    )
```

```python
import functools

import jax
import jax.numpy as jnp
from jax import lax
from jax.experimental import pallas as pl
from jax.experimental.pallas import tpu as pltpu
from jax.sharding import PartitionSpec as P

BF16 = jnp.bfloat16
F32 = jnp.float32
STEPS = (128, 384, 128, 128)
SMEM = pl.BlockSpec(memory_space=pltpu.SMEM)
ANYWHERE = pl.BlockSpec(memory_space=pl.ANY)


def mask_row(masks, tile, extent, width):
    lane = lax.broadcasted_iota(jnp.int32, (1, width), 1)
    row = jnp.zeros((1, width), F32)
    for column in range(width // extent):
        value = masks[tile, column].astype(F32)
        inside = (lane >= column * extent) & (lane < (column + 1) * extent)
        row = jnp.where(inside, value, row)
    return row.astype(BF16)


def aligned(start, size):
    return pl.ds(pl.multiple_of(start, size), size)


def pack_right(target, first, real, imag, sb):
    count = real.shape[0]
    low = first + sb * (first // sb)
    target[aligned(low, count), 0:sb] = real
    target[aligned(low, count), sb : 2 * sb] = imag
    target[aligned(low + sb, count), 0:sb] = -imag
    target[aligned(low + sb, count), sb : 2 * sb] = real


def mask_panel(raw, masks, base, right, turned, sb):
    extent = sb // masks.shape[1]

    @pl.loop(0, raw.shape[1] // extent)
    def tile_step(tile):
        row = mask_row(masks, base + tile, extent, sb)
        first = tile * extent
        real = raw[0, aligned(first, extent), :] * row
        imag = raw[1, aligned(first, extent), :] * row
        pack_right(right, first, real, imag, sb)
        low = first + sb * (first // sb)
        turned[:, aligned(low, extent)] = real.T
        turned[:, aligned(low + sb, extent)] = imag.T


def dot(left, right):
    return jnp.dot(left, right, preferred_element_type=F32)


def row_loop(count, step, body):
    if count == step:
        body(0, pl.ds(0, step))
    else:
        pl.loop(0, count // step)(lambda index: body(index * step, aligned(index * step, step)))


def couple(path, right, packed, level, step, sb):
    size = 2 * sb * level

    def tile_step(first, rows):
        product = dot(path[rows, 0:size], right[...]).astype(BF16)
        real, imag = product[:, 0:sb], product[:, sb : 2 * sb]
        path[rows, size : size + 2 * sb] = -product
        pack_right(packed, first, real, imag, sb)
        low = first + sb * (first // sb)
        path[level * sb : (level + 1) * sb, aligned(low, step)] = -real.T
        path[level * sb : (level + 1) * sb, aligned(low + sb, step)] = -imag.T

    row_loop(level * sb, step, tile_step)


def close(path, turned, packed, corner, level, step, sb):
    size = 2 * sb * level

    def tile_step(first, rows):
        product = dot(turned[rows, :], packed[0:size, :])
        for part in range(2):
            own = product[:, part * sb : (part + 1) * sb] + corner[part, rows, :].astype(F32)
            low = size + part * sb
            path[aligned(level * sb + first, step), low : low + sb] = own.astype(BF16)

    row_loop(sb, step, tile_step)


def leaf_rows(path, m3, x3, target, blocks, shift, weights, running, step, sb):
    weight_imag, weight_real = weights

    def tile_step(first, rows):
        product = dot(path[aligned(shift * sb + first, step), :], m3[...])
        real, imag = product[:, 0:sb], product[:, sb : 2 * sb]
        add_rows(target, rows, -(weight_imag * imag + weight_real * real), running)
        pack_right(x3, shift * sb + first, real.astype(BF16), imag.astype(BF16), sb)

    row_loop(blocks * sb, step, tile_step)


class Copies:
    def __init__(self, sems):
        self.sems = sems
        self.started = {}
        self.count = 0

    def start(self, name, source, target):
        copy = pltpu.make_async_copy(source, target, self.sems.at[self.count])
        self.count += 1
        copy.start()
        self.started.setdefault(name, []).append(copy)

    def wait(self, *names):
        for name in names:
            for copy in self.started.pop(name):
                copy.wait()


def rows_at(index, size):
    return pl.ds(pl.multiple_of(index * size, size), size)


def fetch_root(copies, find, leaf, path, sb):
    for turn in range(8):
        rows = rows_at(leaf ^ turn, sb // 8)
        source = find("root", turn)
        for part in range(2):
            copies.start("root", source.at[part], path.at[rows, part * sb : (part + 1) * sb])


def fetch_pieces(copies, find, leaf, name, turns, target):
    for turn in range(turns):
        size = target.shape[1] // turns
        rows = rows_at((leaf & (turns - 1)) ^ turn, size)
        copies.start(name, find(name, turn), target.at[:, rows, :])


def finder(sources, places):
    def find(name, turn=0):
        operand, index, low, high = places[name][turn]
        source = sources[operand]
        if index is not None:
            source = source.at[index]
        return source if low is None else source.at[:, low:high, :]

    return find


def coordinates(local, per_leaf, pole, weights):
    device = lax.axis_index("wide")
    leaf, member = device // per_leaf, device % per_leaf
    return leaf, weights[member * local + pole, 0], weights[member * local + pole, 1]


def add_rows(out, rows, value, running):
    if running:
        out[rows, :] = out[rows, :] + value
    else:
        out[rows, :] = value


def whole_kernel(sb, step, key, places, running, *refs):
    masks, weights = refs[:2]
    sources, rest = refs[2:-20], refs[-20:]
    upper_out, lower_out, upper, lower, path, w1, e1, w2, e2, w3, e3, m1, m1t, m2, m2t, m3, m3t, x, x3, sems = rest
    leaf, weight_imag, weight_real = coordinates(*key, weights)
    copies = Copies(sems)
    columns = masks.shape[1]
    find = finder(sources, places)
    fetch_root(copies, find, leaf, path, sb)
    fetch_pieces(copies, find, leaf, "w_one", 4, w1)
    fetch_pieces(copies, find, leaf, "e_one", 4, e1)
    fetch_pieces(copies, find, leaf, "w_two", 2, w2)
    copies.start("w_three", find("w_three"), w3)
    fetch_pieces(copies, find, leaf, "e_two", 2, e2)
    if running:
        copies.start("upper", find("upper"), upper)
        copies.start("lower", find("lower"), lower)
    copies.start("e_three", find("e_three"), e3)
    copies.wait("root", "w_one")
    mask_panel(w1, masks, 0, m1, m1t, sb)
    couple(path, m1, x, 1, step, sb)
    copies.wait("e_one", "w_two")
    mask_panel(w2, masks, columns, m2, m2t, sb)
    close(path, m1t, x, e1, 1, step, sb)
    couple(path, m2, x, 2, step, sb)
    copies.wait("w_three", "e_two")
    mask_panel(w3, masks, 3 * columns, m3, m3t, sb)
    close(path, m2t, x, e2, 2, step, sb)
    if running:
        copies.wait("upper")
    leaf_rows(path, m3, x3, upper, 2, 0, (weight_imag, weight_real), running, step, sb)
    copies.start("out", upper, upper_out)
    if running:
        copies.wait("lower")
    leaf_rows(path, m3, x3, lower, 1, 2, (weight_imag, weight_real), running, step, sb)
    copies.start("out", lower.at[0:sb, :], lower_out.at[0:sb, :])
    copies.wait("e_three")

    def last_step(first, rows):
        product = dot(m3t[rows, :], x3[...])
        real = product[:, 0:sb] + e3[0, rows, :].astype(F32)
        imag = product[:, sb : 2 * sb] + e3[1, rows, :].astype(F32)
        add_rows(lower, aligned(sb + first, step), weight_imag * imag + weight_real * real, running)

    row_loop(sb, step, last_step)
    copies.start("out", lower.at[sb:, :], lower_out.at[sb:, :])
    copies.wait("out")


def most_kernel(sb, step, key, places, running, *refs):
    masks, weights = refs[:2]
    sources, rest = refs[2:-25], refs[-25:]
    upper_out, corner_out, low_out, leaf_out, m3_low, m3t_low = rest[:6]
    upper, corner, low_share, leaf_share, path, w1, e1, w2, w3, e3, m1, m1t, m2, m2t, m3, m3t, x, x3, sems = rest[6:]
    leaf, weight_imag, weight_real = coordinates(*key, weights)
    copies = Copies(sems)
    columns = masks.shape[1]
    find = finder(sources, places)
    fetch_root(copies, find, leaf, path, sb)
    fetch_pieces(copies, find, leaf, "w_one", 4, w1)
    fetch_pieces(copies, find, leaf, "e_one", 4, e1)
    fetch_pieces(copies, find, leaf, "w_two", 2, w2)
    copies.start("w_three", find("w_three"), w3)
    if running:
        copies.start("upper", find("upper"), upper)
    copies.start("e_three", find("e_three"), e3)
    copies.wait("root", "w_one")
    mask_panel(w1, masks, 0, m1, m1t, sb)
    couple(path, m1, x, 1, step, sb)
    copies.wait("e_one", "w_two")
    mask_panel(w2, masks, columns, m2, m2t, sb)
    close(path, m1t, x, e1, 1, step, sb)
    couple(path, m2, x, 2, step, sb)
    copies.wait("w_three")
    mask_panel(w3, masks, 3 * columns, m3, m3t, sb)
    copies.start("out", m3.at[4 * sb :, :], m3_low)
    copies.start("out", m3t.at[:, 4 * sb :], m3t_low)

    def corner_step(first, rows):
        corner[rows, :] = dot(m2t[rows, :], x[...])

    row_loop(sb, step, corner_step)
    copies.start("out", corner, corner_out)
    if running:
        copies.wait("upper")
    leaf_rows(path, m3, x3, upper, 2, 0, (weight_imag, weight_real), running, step, sb)
    copies.start("out", upper, upper_out)

    def low_step(first, rows):
        left = path[aligned(2 * sb + first, step), 0 : 4 * sb]
        low_share[rows, :] = dot(left, m3[0 : 4 * sb, :])

    row_loop(sb, step, low_step)
    copies.start("out", low_share, low_out)
    copies.wait("e_three")

    def leaf_step(first, rows):
        product = dot(m3t[rows, 0 : 4 * sb], x3[...])
        for part in range(2):
            where = slice(part * sb, (part + 1) * sb)
            leaf_share[rows, where] = product[:, where] + e3[part, rows, :].astype(F32)

    row_loop(sb, step, leaf_step)
    copies.start("out", leaf_share, leaf_out)
    copies.wait("out")


def corner_kernel(sb, key, places, *refs):
    weights = refs[0]
    sources, rest = refs[1:-11], refs[-11:]
    lower_out, lower, e2, corner, low_share, leaf_share, m3_low, m3t_low, left, x3, sems = rest
    leaf, weight_imag, weight_real = coordinates(*key, weights)
    copies = Copies(sems)
    find = finder(sources, places)
    fetch_pieces(copies, find, leaf, "e_two", 2, e2)
    copies.start("corner", find("corner"), corner)
    copies.start("low", find("m3_low"), m3_low)
    copies.start("low", find("low_share"), low_share)
    copies.start("leaf", find("m3t_low"), m3t_low)
    copies.start("leaf", find("leaf_share"), leaf_share)
    copies.wait("e_two", "corner")
    for part in range(2):
        where = slice(part * sb, (part + 1) * sb)
        left[:, where] = (corner[:, where] + e2[part].astype(F32)).astype(BF16)
    copies.wait("low")
    product = low_share[...] + dot(left[...], m3_low[...])
    real, imag = product[:, 0:sb], product[:, sb : 2 * sb]
    lower[0:sb, :] = -(weight_imag * imag + weight_real * real)
    pack_right(x3, 0, real.astype(BF16), imag.astype(BF16), sb)
    copies.start("out", lower.at[0:sb, :], lower_out.at[0:sb, :])
    copies.wait("leaf")
    product = leaf_share[...] + dot(m3t_low[...], x3[...])
    real, imag = product[:, 0:sb], product[:, sb : 2 * sb]
    lower[sb : 2 * sb, :] = weight_imag * imag + weight_real * real
    copies.start("out", lower.at[sb:, :], lower_out.at[sb:, :])
    copies.wait("out")


def call(kernel, name, scalars, pieces, outs, scratch, flops):
    sources, places = [], {}

    def operand(array):
        for index, known in enumerate(sources):
            if known is array:
                return index
        sources.append(array)
        return len(sources) - 1

    for key, turns in pieces.items():
        places[key] = {turn: (operand(piece[0]), *piece[1:]) for turn, piece in turns.items()}
    results = [jax.ShapeDtypeStruct(shape, kind) for shape, kind, _ in outs]
    return pl.pallas_call(
        kernel(places),
        out_shape=results,
        in_specs=[SMEM] * len(scalars) + [ANYWHERE] * len(sources),
        out_specs=[spec for _, _, spec in outs],
        scratch_shapes=[pltpu.VMEM(shape, kind) for shape, kind in scratch]
        + [pltpu.SemaphoreType.DMA((40,))],
        compiler_params=pltpu.CompilerParams(vmem_limit_bytes=60 << 20),
        cost_estimate=pl.CostEstimate(flops=flops, bytes_accessed=1 << 20, transcendentals=0),
        name=name,
    )(*scalars, *sources)


def shards(
    root_band,
    w_one,
    e_one,
    w_two,
    e_two,
    w_three,
    e_three,
    mask_one,
    mask_two,
    mask_three,
    pole_weights,
):
    devices = lax.axis_size("wide")
    per_leaf = devices // 8
    device_index = lax.axis_index("wide")
    leaf = device_index // per_leaf
    member = device_index % per_leaf
    local = root_band.shape[0]
    sb = w_three.shape[-1]
    quarter, half = sb // 4, sb // 2
    last = local - 1

    def turn(block, bits, *after):
        after = [array for array in after if array is not None]
        if after:
            block = lax.optimization_barrier((block, *after))[0]
        route = [(low, low ^ bits * per_leaf) for low in range(devices)]
        return lax.ppermute(block, "wide", route)

    early = (local + 1) // 2
    batches = [slice(0, early)] + ([slice(early, local)] if local > early else [])
    late = len(batches) > 1
    packs = [jnp.concatenate([w_one[batch], e_one[batch]], axis=2) for batch in batches]
    panels = [jnp.concatenate([w_two[pole], e_two[pole]], axis=1) for pole in range(last)]

    root = {0: root_band, 1: turn(root_band, 1)}
    root[2], root[6] = turn(root_band, 2), turn(root_band, 6)
    one = [{1: turn(packs[0], 1), 2: turn(packs[0], 2)}]
    two = []
    if last > 0:
        two.append(turn(panels[0], 1, root[1]))
    root[4] = turn(root_band, 4, root[2])
    root[7] = turn(root[1], 6, root[6])
    root[5] = turn(root[1], 4, one[0][2])
    root[3] = turn(root[1], 2, root[4])
    if late:
        one.append({1: turn(packs[1], 1, one[0][1])})
    one[0][3] = turn(one[0][1], 2, root[7])
    if last > 1:
        two.append(turn(panels[1], 1, two[0]))
    if late:
        one[1][2] = turn(packs[1], 2, root[5])
        one[1][3] = turn(one[1][1], 2, root[3])
    if last > 2:
        two.append(turn(panels[2], 1, one[1][1]))
    last_two = turn(w_two[last], 1, one[0][3], *two[1:2])

    masks = jnp.concatenate(
        [
            lax.dynamic_index_in_dim(mask_one, leaf // 4, 0, keepdims=False),
            lax.dynamic_index_in_dim(mask_two, leaf // 2, 0, keepdims=False),
            lax.dynamic_index_in_dim(mask_three, leaf, 0, keepdims=False),
        ],
        axis=0,
    )
    upper = lower = None
    single = lambda array, index=None: {0: (array, index, None, None)}
    unit = 2 * sb**3
    for pole in range(local):
        batch = 0 if pole < early else 1
        at = pole - batches[batch].start
        pieces = {"root": {bits: (root[bits], pole, None, None) for bits in range(8)}}
        pieces["w_one"], pieces["e_one"] = single(w_one, pole), single(e_one, pole)
        for bits in (1, 2, 3):
            pieces["w_one"][bits] = (one[batch][bits], at, 0, quarter)
            pieces["e_one"][bits] = (one[batch][bits], at, quarter, 2 * quarter)
        pieces["w_three"], pieces["e_three"] = single(w_three, pole), single(e_three, pole)
        key = (local, per_leaf, pole)
        running = upper is not None
        if running:
            pieces["upper"] = single(upper)
        halves = [((2 * sb, sb), F32)]
        shares = [((sb, 2 * sb), F32)] * 3
        raw = [((2, sb, sb), BF16)]
        packed = [
            ((2 * sb, 2 * sb), BF16),
            ((sb, 2 * sb), BF16),
            ((4 * sb, 2 * sb), BF16),
            ((sb, 4 * sb), BF16),
            ((6 * sb, 2 * sb), BF16),
            ((sb, 6 * sb), BF16),
            ((4 * sb, 2 * sb), BF16),
        ]
        path = [((3 * sb, 6 * sb), BF16)]
        two_raw, three_raw = [((2, 2 * sb, sb), BF16)], [((2, 3 * sb, sb), BF16)]
        if pole < last:
            pieces["w_two"] = {**single(w_two, pole), 1: (two[pole], None, 0, sb)}
            pieces["e_two"] = {**single(e_two, pole), 1: (two[pole], None, sb, sb + half)}
            if running:
                pieces["lower"] = single(lower)
            upper, lower = call(
                lambda places: functools.partial(whole_kernel, sb, STEPS[pole % len(STEPS)], key, places, running),
                "pole_" + str(pole),
                [masks, pole_weights],
                pieces,
                [((2 * sb, sb), F32, ANYWHERE), ((2 * sb, sb), F32, ANYWHERE)],
                halves * 2 + path + raw * 2 + two_raw + raw + three_raw + raw + packed
                + [((6 * sb, 2 * sb), BF16)],
                80 * unit,
                )
            if pole == min(1, last - 1):
                last_corner = turn(e_two[last], 1, lower)
            continue
        if local == 1:
            last_corner = turn(e_two[last], 1)
        pieces["w_two"] = {**single(w_two, pole), 1: (last_two, None, None, None)}
        upper, *between = call(
            lambda places: functools.partial(most_kernel, sb, STEPS[-1], key, places, running),
            "pole_most",
            [masks, pole_weights],
            pieces,
            [((2 * sb, sb), F32, ANYWHERE)]
            + [((sb, 2 * sb), F32, ANYWHERE)] * 3
            + [((2 * sb, 2 * sb), BF16, ANYWHERE), ((sb, 2 * sb), BF16, ANYWHERE)],
            halves + shares + path + raw * 2 + two_raw + three_raw + raw + packed
            + [((4 * sb, 2 * sb), BF16)],
            72 * unit,
        )
        names = ("corner", "low_share", "leaf_share", "m3_low", "m3t_low")
        pieces = {name: single(array) for name, array in zip(names, between)}
        pieces["e_two"] = {**single(e_two, pole), 1: (last_corner, None, None, None)}
        (corner_rows,) = call(
            lambda places: functools.partial(corner_kernel, sb, key, places),
            "pole_corner",
            [pole_weights],
            pieces,
            [((2 * sb, sb), F32, ANYWHERE)],
            halves + raw + shares
            + [((2 * sb, 2 * sb), BF16)] + [((sb, 2 * sb), BF16)] * 2 + [((2 * sb, 2 * sb), BF16)],
            8 * unit,
        )

    if per_leaf == 1:
        if lower is not None:
            corner_rows = lower + corner_rows
        return jnp.concatenate([upper, corner_rows], axis=0)
    bit = per_leaf // 2
    low_members = [low for low in range(devices) if low & bit == 0]
    to_low = [(low | bit, low) for low in low_members]
    to_high = [(low, low | bit) for low in low_members]
    is_low = member & bit == 0
    upper = upper + lax.ppermute(upper, "wide", to_low)
    if lower is None:
        early_rows = jnp.where(is_low, upper, 0.0)
    else:
        early_rows = jnp.where(is_low, upper, lower + lax.ppermute(lower, "wide", to_high))
    early_rows = lax.optimization_barrier(early_rows)
    late_rows = corner_rows + lax.ppermute(corner_rows, "wide", to_high)
    density = early_rows + jnp.where(is_low, 0.0, late_rows)
    while bit > 1:
        bit //= 2
        half_count = density.shape[0] // 2
        bit_set = member & bit != 0
        kept = jnp.where(bit_set, density[half_count:], density[:half_count])
        sent = jnp.where(bit_set, density[:half_count], density[half_count:])
        density = kept + lax.ppermute(sent, "wide", [(low, low ^ bit) for low in range(devices)])
    return density


def solution(mesh):
    split = P(("groups", "wide"), None, None, None)
    return jax.shard_map(
        shards,
        mesh=mesh,
        in_specs=(split,) * 7 + (P("groups", None, None),) * 3 + (P(),),
        out_specs=P(("groups", "wide"), None),
        check_vma=False,
    )
```

```python
import functools

import jax
import jax.numpy as jnp
from jax import lax
from jax.experimental import pallas as pl
from jax.experimental.pallas import tpu as pltpu
from jax.sharding import PartitionSpec as P

BF16 = jnp.bfloat16
F32 = jnp.float32
SMEM = pl.BlockSpec(memory_space=pltpu.SMEM)
ANYWHERE = pl.BlockSpec(memory_space=pl.ANY)
WHOLE = pl.BlockSpec(memory_space=pltpu.VMEM)


def mask_row(masks, tile, extent, width):
    lane = lax.broadcasted_iota(jnp.int32, (1, width), 1)
    row = jnp.zeros((1, width), F32)
    for column in range(width // extent):
        value = masks[tile, column].astype(F32)
        inside = (lane >= column * extent) & (lane < (column + 1) * extent)
        row = jnp.where(inside, value, row)
    return row.astype(BF16)


def right_form(target, value, sb):
    real, imag = value[:, 0:sb], value[:, sb : 2 * sb]
    target[0:sb, 0:sb] = real
    target[0:sb, sb : 2 * sb] = imag
    target[sb : 2 * sb, 0:sb] = -imag
    target[sb : 2 * sb, sb : 2 * sb] = real


def turned_form(target, low, real, imag, sb):
    target[0:sb, low : low + sb] = real
    target[0:sb, low + sb : low + 2 * sb] = -imag
    target[sb : 2 * sb, low : low + sb] = imag
    target[sb : 2 * sb, low + sb : low + 2 * sb] = real


def mask_panel(raw, masks, right, turned, sb):
    extent = sb // masks.shape[1]
    for tile in range(raw.shape[1] // extent):
        row = mask_row(masks, tile, extent, sb)
        first = tile * extent
        rows = slice(first, first + extent)
        real = raw[0, rows, :] * row
        imag = raw[1, rows, :] * row
        right[rows, 0:sb] = real
        right[rows, sb : 2 * sb] = imag
        right[sb + first : sb + first + extent, 0:sb] = -imag
        right[sb + first : sb + first + extent, sb : 2 * sb] = real
        turned[:, rows] = real.T
        turned[:, sb + first : sb + first + extent] = imag.T


def dot(left, right):
    return jnp.dot(left, right, preferred_element_type=F32)


def dot_turned(left, right):
    return lax.dot_general(left, right, (((1,), (1,)), ((), ())), preferred_element_type=F32)


def negated(product):
    return (-product).astype(BF16)


def weigh(product, weights, sb):
    weight_imag, weight_real = weights
    return weight_imag * product[:, sb : 2 * sb] + weight_real * product[:, 0:sb]


def parts(value, sb):
    return value[:, 0:sb], value[:, sb : 2 * sb]


def with_corner(corner, product, sb):
    both = jnp.concatenate([corner[0].astype(F32), corner[1].astype(F32)], axis=1)
    return both + product


class Copies:
    def __init__(self, sems):
        self.sems = sems
        self.started = {}
        self.count = 0

    def start(self, name, source, target):
        copy = pltpu.make_async_copy(source, target, self.sems.at[self.count])
        self.count += 1
        copy.start()
        self.started.setdefault(name, []).append(copy)

    def wait(self, *names):
        for name in names:
            for copy in self.started.pop(name):
                copy.wait()


def rows_at(index, size):
    return pl.ds(pl.multiple_of(index * size, size), size)


def fetch_root(copies, find, leaf, path, sb):
    for turn in range(8):
        rows = rows_at(leaf ^ turn, sb // 8)
        source = find("root", turn)
        for part in range(2):
            copies.start("root", source.at[part], path.at[rows, part * sb : (part + 1) * sb])


def fetch_pieces(copies, find, leaf, name, turns, target):
    for turn in range(turns):
        size = target.shape[1] // turns
        rows = rows_at((leaf & (turns - 1)) ^ turn, size)
        copies.start(name, find(name, turn), target.at[:, rows, :])


def finder(sources, places):
    def find(name, turn=0):
        operand, index, low, high = places[name][turn]
        source = sources[operand]
        if index is not None:
            source = source.at[index]
        return source if low is None else source.at[:, low:high, :]

    return find


def coordinates(local, per_leaf, pole, weights):
    device = lax.axis_index("wide")
    leaf, member = device // per_leaf, device % per_leaf
    return leaf, (weights[member * local + pole, 0], weights[member * local + pole, 1])


def add_rows(out, rows, value, running):
    if running:
        out[rows, :] = out[rows, :] + value
    else:
        out[rows, :] = value


def fetch_turned(copies, find, leaf, target, sb):
    for turn in range(2):
        for part in range(2):
            low = ((leaf & 1) ^ turn) * 2 * sb + part * sb
            columns = pl.ds(pl.multiple_of(low, sb), sb)
            copies.start("w_two", find("w_two", turn).at[part], target.at[:, columns])


def panel_kernel(sb, pole, per_leaf, with_block, masks, w_two, *refs):
    out, raw, sems = refs[-3:]
    copies = Copies(sems)
    copies.start("w", w_two.at[pole], raw)
    if with_block:
        copies.start("e", refs[0].at[pole], out.at[:, sb:, :])
    columns = masks.shape[1]
    extent = sb // columns
    half = (lax.axis_index("wide") // per_leaf) & 1
    copies.wait("w")
    for tile in range(columns):
        row = mask_row(masks, columns + half * columns + tile, extent, sb)
        rows = slice(tile * extent, (tile + 1) * extent)
        for part in range(2):
            out[part, 0:sb, rows] = (raw[part, rows, :] * row).T
    if with_block:
        copies.wait("e")


def leaf_panel_kernel(sb, pole, masks, w_three, out, raw, sems):
    copies = Copies(sems)
    copies.start("w", w_three.at[pole], raw)
    columns = masks.shape[1]
    extent = sb // columns
    copies.wait("w")
    for tile in range(3 * columns):
        row = mask_row(masks, 3 * columns + tile, extent, sb)
        rows = slice(tile * extent, (tile + 1) * extent)
        low = 2 * sb * (tile // columns) + (tile % columns) * extent
        for part in range(2):
            out[:, low + part * sb : low + part * sb + extent] = (raw[part, rows, :] * row).T


def level_two(copies, state, e1, m1, m1t, m2n, h1n, sb):
    w1, masks, path, m2t, x1, x2t, x2b, low_form = state
    size = 2 * sb
    copies.wait("root", "w_one")
    mask_panel(w1, masks, m1, m1t, sb)
    value = negated(dot(path[:, 0:size], m1[...]))
    path[:, size : 2 * size] = value
    right_form(x1, value, sb)
    copies.wait("e_one", "w_two")
    for block in range(2):
        low = block * size
        turned_form(m2n, low, m2t[:, low : low + sb], m2t[:, low + sb : low + size], sb)
    value = with_corner(e1, -dot(m1t[...], x1[...]), sb).astype(BF16)
    turned_form(h1n, 0, *parts(value, sb), sb)
    value = negated(dot_turned(path[:, 0 : 2 * size], m2n[...]))
    path[:, 2 * size :] = value
    right_form(x2t, value, sb)
    value = negated(dot(m2t[:, 0:size], x1[...]) + dot_turned(m2t[:, size:], h1n[...]))
    right_form(x2b, value, sb)
    turned_form(low_form, 0, *parts(value, sb), sb)
    return dot(m2t[:, 0:size], x2t[...]) + dot_turned(m2t[:, size:], low_form[:, 0:size])


def whole_kernel(sb, key, places, running, turn_back, *refs):
    masks, weights = refs[:2]
    sources, rest = refs[2:-23], refs[-23:]
    upper_out, lower_out, upper, lower, path, w1, e1, e2, e3, m1, m1t, m2t, m2n, m3t, m3n = rest[:15]
    x1, h1n, x2t, x2b, low_form, r3t, r3n, sems = rest[15:]
    leaf, weigh_by = coordinates(*key, weights)
    copies = Copies(sems)
    size = 2 * sb
    find = finder(sources, places)
    fetch_root(copies, find, leaf, path, sb)
    fetch_pieces(copies, find, leaf, "w_one", 4, w1)
    fetch_pieces(copies, find, leaf, "e_one", 4, e1)
    fetch_turned(copies, find, leaf, m2t, sb)
    copies.start("m_three", find("m_three"), m3t)
    fetch_pieces(copies, find, leaf, "e_two", 2, e2)
    if running:
        copies.start("total", find("upper"), upper)
        copies.start("total", find("lower"), lower)
    copies.start("e_three", find("e_three"), e3)
    taken = level_two(copies, (w1, masks, path, m2t, x1, x2t, x2b, low_form), e1, m1, m1t, m2n, h1n, sb)
    copies.wait("m_three", "e_two")
    value = with_corner(e2, -taken, sb).astype(BF16)
    turned_form(low_form, size, *parts(value, sb), sb)
    for block in range(3):
        low = block * size
        turned_form(m3n, low, m3t[:, low : low + sb], m3t[:, low + sb : low + size], sb)
    if running:
        copies.wait("total")
    product = dot_turned(path[...], m3n[...])
    add_rows(upper, slice(0, sb), -weigh(product, weigh_by, sb), running)
    right_form(r3t, product.astype(BF16), sb)
    product = dot(m3t[:, 0:size], x1[...]) + dot_turned(m3t[:, size : 2 * size], h1n[...])
    product = product + dot(m3t[:, 2 * size :], x2b[...])
    add_rows(upper, slice(sb, size), -weigh(product, weigh_by, sb), running)
    turned_form(r3n, 0, *parts(product.astype(BF16), sb), sb)
    copies.start("out", upper, upper_out)
    product = dot(m3t[:, 0:size], x2t[...]) + dot_turned(m3t[:, size:], low_form[...])
    add_rows(lower, slice(0, sb), -weigh(product, weigh_by, sb), running)
    turned_form(r3n, size, *parts(product.astype(BF16), sb), sb)
    if turn_back:
        lower[0:sb, :] = lower[0:sb, :].T
    copies.start("out", lower.at[0:sb, :], lower_out.at[0:sb, :])
    copies.wait("e_three")
    product = dot(m3t[:, 0:size], r3t[...]) + dot_turned(m3t[:, size:], r3n[...])
    product = with_corner(e3, product, sb)
    add_rows(lower, slice(sb, size), weigh(product, weigh_by, sb), running)
    copies.start("out", lower.at[sb:, :], lower_out.at[sb:, :])
    copies.wait("out")


def most_kernel(sb, key, places, running, *refs):
    masks, weights = refs[:2]
    sources, rest = refs[2:-26], refs[-26:]
    upper_out, taken_out, low_out, leaf_out, upper, taken, low_share, leaf_share = rest[:8]
    path, w1, e1, e3, m1, m1t, m2t, m2n, m3t, m3n, x1, h1n, x2t, x2b, low_form, r3t, r3n, sems = rest[8:]
    leaf, weigh_by = coordinates(*key, weights)
    copies = Copies(sems)
    size = 2 * sb
    find = finder(sources, places)
    fetch_root(copies, find, leaf, path, sb)
    fetch_pieces(copies, find, leaf, "w_one", 4, w1)
    fetch_pieces(copies, find, leaf, "e_one", 4, e1)
    fetch_turned(copies, find, leaf, m2t, sb)
    copies.start("m_three", find("m_three"), m3t)
    if running:
        copies.start("total", find("upper"), upper)
    copies.start("e_three", find("e_three"), e3)
    taken[...] = level_two(
        copies, (w1, masks, path, m2t, x1, x2t, x2b, low_form), e1, m1, m1t, m2n, h1n, sb
    )
    copies.start("out", taken, taken_out)
    copies.wait("m_three")
    for block in range(3):
        low = block * size
        turned_form(m3n, low, m3t[:, low : low + sb], m3t[:, low + sb : low + size], sb)
    low_share[...] = dot(m3t[:, 0:size], x2t[...]) + dot_turned(m3t[:, size : 2 * size], low_form[...])
    copies.start("out", low_share, low_out)
    if running:
        copies.wait("total")
    product = dot_turned(path[...], m3n[...])
    add_rows(upper, slice(0, sb), -weigh(product, weigh_by, sb), running)
    right_form(r3t, product.astype(BF16), sb)
    product = dot(m3t[:, 0:size], x1[...]) + dot_turned(m3t[:, size : 2 * size], h1n[...])
    product = product + dot(m3t[:, 2 * size :], x2b[...])
    add_rows(upper, slice(sb, size), -weigh(product, weigh_by, sb), running)
    upper[sb:size, :] = upper[sb:size, :].T
    turned_form(r3n, 0, *parts(product.astype(BF16), sb), sb)
    copies.start("out", upper, upper_out)
    copies.wait("e_three")
    product = dot(m3t[:, 0:size], r3t[...]) + dot_turned(m3t[:, size : 2 * size], r3n[...])
    leaf_share[...] = with_corner(e3, product, sb)
    copies.start("out", leaf_share, leaf_out)
    copies.wait("out")


def corner_kernel(sb, key, places, *refs):
    weights = refs[0]
    sources, rest = refs[1:-10], refs[-10:]
    lower_out, lower, e2, taken, low_share, leaf_share, m3t, h2n, r3n, sems = rest
    leaf, weigh_by = coordinates(*key, weights)
    copies = Copies(sems)
    find = finder(sources, places)
    fetch_pieces(copies, find, leaf, "e_two", 2, e2)
    copies.start("taken", find("taken"), taken)
    copies.start("low", find("m_three").at[:, 4 * sb :], m3t)
    copies.start("low", find("low_share"), low_share)
    copies.start("leaf", find("leaf_share"), leaf_share)
    copies.wait("e_two", "taken")
    value = with_corner(e2, -taken[...], sb).astype(BF16)
    turned_form(h2n, 0, *parts(value, sb), sb)
    copies.wait("low")
    product = low_share[...] + dot_turned(m3t[...], h2n[...])
    turned_form(r3n, 0, *parts(product.astype(BF16), sb), sb)
    lower[0:sb, :] = -weigh(product, weigh_by, sb).T
    copies.start("out", lower.at[0:sb, :], lower_out.at[0:sb, :])
    copies.wait("leaf")
    product = leaf_share[...] + dot_turned(m3t[...], r3n[...])
    lower[sb : 2 * sb, :] = weigh(product, weigh_by, sb)
    copies.start("out", lower.at[sb:, :], lower_out.at[sb:, :])
    copies.wait("out")


def call(kernel, name, scalars, pieces, outs, scratch, flops):
    sources, places = [], {}

    def operand(array):
        for index, known in enumerate(sources):
            if known is array:
                return index
        sources.append(array)
        return len(sources) - 1

    for key, turns in pieces.items():
        places[key] = {turn: (operand(piece[0]), *piece[1:]) for turn, piece in turns.items()}
    results = [jax.ShapeDtypeStruct(shape, kind) for shape, kind, _ in outs]
    return pl.pallas_call(
        kernel(places),
        out_shape=results,
        in_specs=[SMEM] * len(scalars) + [ANYWHERE] * len(sources),
        out_specs=[spec for _, _, spec in outs],
        scratch_shapes=[pltpu.VMEM(shape, kind) for shape, kind in scratch]
        + [pltpu.SemaphoreType.DMA((40,))],
        compiler_params=pltpu.CompilerParams(vmem_limit_bytes=60 << 20),
        cost_estimate=pl.CostEstimate(flops=flops, bytes_accessed=1 << 20, transcendentals=0),
        name=name,
    )(*scalars, *sources)


def shards(
    root_band,
    w_one,
    e_one,
    w_two,
    e_two,
    w_three,
    e_three,
    mask_one,
    mask_two,
    mask_three,
    pole_weights,
):
    devices = lax.axis_size("wide")
    per_leaf = devices // 8
    device_index = lax.axis_index("wide")
    leaf = device_index // per_leaf
    member = device_index % per_leaf
    local = root_band.shape[0]
    sb = w_three.shape[-1]
    quarter, half = sb // 4, sb // 2
    last = local - 1

    def turn(block, bits, *after):
        after = [array for array in after if array is not None]
        if after:
            block = lax.optimization_barrier((block, *after))[0]
        route = [(low, low ^ bits * per_leaf) for low in range(devices)]
        return lax.ppermute(block, "wide", route)

    early = (local + 1) // 2
    batches = [slice(0, early)] + ([slice(early, local)] if local > early else [])
    late = len(batches) > 1
    packs = [jnp.concatenate([w_one[batch], e_one[batch]], axis=2) for batch in batches]
    masks = jnp.concatenate(
        [
            lax.dynamic_index_in_dim(mask_one, leaf // 4, 0, keepdims=False),
            lax.dynamic_index_in_dim(mask_two, leaf // 2, 0, keepdims=False),
            lax.dynamic_index_in_dim(mask_three, leaf, 0, keepdims=False),
        ],
        axis=0,
    )
    single = lambda array, index=None: {0: (array, index, None, None)}
    panels, leaf_panels = [], []
    unit = 2 * sb**3
    for pole in range(local):
        pair = pole < last
        panels += call(
            lambda places: functools.partial(panel_kernel, sb, pole, per_leaf, pair),
            "panel_" + str(pole),
            [masks],
            {"w_two": single(w_two), **({"e_two": single(e_two)} if pair else {})},
            [((2, sb + half if pair else sb, sb), BF16, WHOLE)],
            [((2, sb, sb), BF16)],
            2 * unit,
        )
        leaf_panels += call(
            lambda places: functools.partial(leaf_panel_kernel, sb, pole),
            "leaf_panel_" + str(pole),
            [masks],
            {"w_three": single(w_three)},
            [((sb, 6 * sb), BF16, WHOLE)],
            [((2, 3 * sb, sb), BF16)],
            4 * unit,
        )

    root = {0: root_band, 1: turn(root_band, 1)}
    root[2], root[6] = turn(root_band, 2), turn(root_band, 6)
    one = [{1: turn(packs[0], 1), 2: turn(packs[0], 2)}]
    two = []
    if last > 0:
        two.append(turn(panels[0], 1, root[1]))
    root[4] = turn(root_band, 4, root[2])
    root[7] = turn(root[1], 6, root[6])
    root[5] = turn(root[1], 4, one[0][2])
    root[3] = turn(root[1], 2, root[4])
    if late:
        one.append({1: turn(packs[1], 1, one[0][1])})
    one[0][3] = turn(one[0][1], 2, root[7])
    if last > 1:
        two.append(turn(panels[1], 1, two[0]))
    if late:
        one[1][2] = turn(packs[1], 2, root[5])
        one[1][3] = turn(one[1][1], 2, root[3])
    if last > 2:
        two.append(turn(panels[2], 1, one[1][1]))
    last_two = turn(panels[last], 1, one[0][3], *two[1:2])

    upper = lower = None
    for pole in range(local):
        batch = 0 if pole < early else 1
        at = pole - batches[batch].start
        pieces = {"root": {bits: (root[bits], pole, None, None) for bits in range(8)}}
        pieces["w_one"], pieces["e_one"] = single(w_one, pole), single(e_one, pole)
        for bits in (1, 2, 3):
            pieces["w_one"][bits] = (one[batch][bits], at, 0, quarter)
            pieces["e_one"][bits] = (one[batch][bits], at, quarter, 2 * quarter)
        pieces["m_three"], pieces["e_three"] = single(leaf_panels[pole]), single(e_three, pole)
        key = (local, per_leaf, pole)
        running = upper is not None
        if running:
            pieces["upper"] = single(upper)
        halves = [((2 * sb, sb), F32)]
        shares = [((sb, 2 * sb), F32)] * 3
        raw = [((2, sb, sb), BF16)]
        path = [((sb, 6 * sb), BF16)]
        square, flat = ((2 * sb, 2 * sb), BF16), ((sb, 2 * sb), BF16)
        panel_forms = [square, flat, ((sb, 4 * sb), BF16), ((2 * sb, 4 * sb), BF16)]
        panel_forms += [((sb, 6 * sb), BF16), ((2 * sb, 6 * sb), BF16)]
        double = ((2 * sb, 4 * sb), BF16)
        if pole < last:
            pieces["w_two"] = {0: (panels[pole], None, 0, sb), 1: (two[pole], None, 0, sb)}
            pieces["e_two"] = {**single(e_two, pole), 1: (two[pole], None, sb, sb + half)}
            if running:
                pieces["lower"] = single(lower)
            upper, lower = call(
                lambda places: functools.partial(whole_kernel, sb, key, places, running, pole == last - 1),
                "pole_" + str(pole),
                [masks, pole_weights],
                pieces,
                [((2 * sb, sb), F32, ANYWHERE), ((2 * sb, sb), F32, ANYWHERE)],
                halves * 2 + path + raw * 4 + panel_forms + [square] * 4 + [double, square, double],
                80 * unit,
                )
            if pole == min(1, last - 1):
                last_corner = turn(e_two[last], 1, lower)
            continue
        if local == 1:
            last_corner = turn(e_two[last], 1)
        pieces["w_two"] = {**single(panels[pole]), 1: (last_two, None, None, None)}
        upper, *between = call(
            lambda places: functools.partial(most_kernel, sb, key, places, running),
            "pole_most",
            [masks, pole_weights],
            pieces,
            [((2 * sb, sb), F32, ANYWHERE)] + [((sb, 2 * sb), F32, ANYWHERE)] * 3,
            halves + shares + path + raw * 3 + panel_forms + [square] * 7,
            72 * unit,
        )
        names = ("taken", "low_share", "leaf_share")
        pieces = {name: single(array) for name, array in zip(names, between)}
        pieces["m_three"] = single(leaf_panels[pole])
        pieces["e_two"] = {**single(e_two, pole), 1: (last_corner, None, None, None)}
        (corner_rows,) = call(
            lambda places: functools.partial(corner_kernel, sb, key, places),
            "pole_corner",
            [pole_weights],
            pieces,
            [((2 * sb, sb), F32, ANYWHERE)],
            halves + raw + shares + [flat] + [square] * 2,
            8 * unit,
        )

    if per_leaf == 1:
        if lower is not None:
            corner_rows = lower + corner_rows
        return jnp.concatenate([upper, corner_rows], axis=0)
    bit = per_leaf // 2
    low_members = [low for low in range(devices) if low & bit == 0]
    to_low = [(low | bit, low) for low in low_members]
    to_high = [(low, low | bit) for low in low_members]
    is_low = member & bit == 0
    upper = upper + lax.ppermute(upper, "wide", to_low)
    if lower is None:
        early_rows = jnp.where(is_low, upper, 0.0)
    else:
        early_rows = jnp.where(is_low, upper, lower + lax.ppermute(lower, "wide", to_high))
    early_rows = lax.optimization_barrier(early_rows)
    late_rows = corner_rows + lax.ppermute(corner_rows, "wide", to_high)
    density = early_rows + jnp.where(is_low, 0.0, late_rows)
    while bit > 1:
        bit //= 2
        half_count = density.shape[0] // 2
        bit_set = member & bit != 0
        kept = jnp.where(bit_set, density[half_count:], density[:half_count])
        sent = jnp.where(bit_set, density[:half_count], density[half_count:])
        density = kept + lax.ppermute(sent, "wide", [(low, low ^ bit) for low in range(devices)])
    return density


def solution(mesh):
    split = P(("groups", "wide"), None, None, None)
    return jax.shard_map(
        shards,
        mesh=mesh,
        in_specs=(split,) * 7 + (P("groups", None, None),) * 3 + (P(),),
        out_specs=P(("groups", "wide"), None),
        check_vma=False,
    )
```

```python
import functools

import jax
import jax.numpy as jnp
from jax import lax
from jax.experimental import pallas as pl
from jax.experimental.pallas import tpu as pltpu
from jax.sharding import PartitionSpec as P

BF16 = jnp.bfloat16
F32 = jnp.float32
SMEM = pl.BlockSpec(memory_space=pltpu.SMEM)
ANYWHERE = pl.BlockSpec(memory_space=pl.ANY)


def mask_row(masks, tile, extent, width):
    lane = lax.broadcasted_iota(jnp.int32, (1, width), 1)
    row = jnp.zeros((1, width), F32)
    for column in range(width // extent):
        value = masks[tile, column].astype(F32)
        inside = (lane >= column * extent) & (lane < (column + 1) * extent)
        row = jnp.where(inside, value, row)
    return row.astype(BF16)


def aligned(start, size):
    return pl.ds(start if isinstance(start, int) else pl.multiple_of(start, size), size)


def pack_right(target, first, real, imag, sb):
    count = real.shape[0]
    low = first + sb * (first // sb)
    target[aligned(low, count), 0:sb] = real
    target[aligned(low, count), sb : 2 * sb] = imag
    target[aligned(low + sb, count), 0:sb] = -imag
    target[aligned(low + sb, count), sb : 2 * sb] = real


def mask_panel(raw, masks, base, right, turned, sb):
    columns = masks.shape[1]
    extent = sb // columns
    blocks = raw.shape[1] // sb

    def block_step(block):
        for tile in range(columns):
            row = mask_row(masks, base + block * columns + tile, extent, sb)
            rows = aligned(block * sb + tile * extent, extent)
            real = raw[0, rows, :] * row
            imag = raw[1, rows, :] * row
            low = block * 2 * sb + tile * extent
            right[aligned(low, extent), 0:sb] = real
            right[aligned(low, extent), sb : 2 * sb] = imag
            right[aligned(low + sb, extent), 0:sb] = -imag
            right[aligned(low + sb, extent), sb : 2 * sb] = real
            turned[:, aligned(low, extent)] = real.T
            turned[:, aligned(low + sb, extent)] = imag.T

    if blocks > 2:
        pl.loop(0, blocks)(block_step)
    else:
        for block in range(blocks):
            block_step(block)


def dot(left, right):
    return jnp.dot(left, right, preferred_element_type=F32)


def couple(path, right, packed, level, sb):
    size = 2 * sb * level
    for block in range(level):
        rows = slice(block * sb, (block + 1) * sb)
        product = dot(path[rows, 0:size], right[...]).astype(BF16)
        real, imag = product[:, 0:sb], product[:, sb : 2 * sb]
        path[rows, size : size + 2 * sb] = -product
        pack_right(packed, block * sb, real, imag, sb)
        low = 2 * sb * block
        path[level * sb : (level + 1) * sb, low : low + sb] = -real.T
        path[level * sb : (level + 1) * sb, low + sb : low + 2 * sb] = -imag.T


def close(path, product, corner, level, sb):
    rows = slice(level * sb, (level + 1) * sb)
    for part in range(2):
        own = product[:, part * sb : (part + 1) * sb] + corner[part].astype(F32)
        low = 2 * sb * level + part * sb
        path[rows, low : low + sb] = own.astype(BF16)


class Copies:
    def __init__(self, sems):
        self.sems = sems
        self.started = {}
        self.count = 0

    def start(self, name, source, target):
        copy = pltpu.make_async_copy(source, target, self.sems.at[self.count])
        self.count += 1
        copy.start()
        self.started.setdefault(name, []).append(copy)

    def wait(self, *names):
        for name in names:
            for copy in self.started.pop(name):
                copy.wait()


def rows_at(index, size):
    return pl.ds(pl.multiple_of(index * size, size), size)


def fetch_root(copies, find, leaf, path, sb):
    for turn in range(8):
        rows = rows_at(leaf ^ turn, sb // 8)
        source = find("root", turn)
        for part in range(2):
            copies.start("root", source.at[part], path.at[rows, part * sb : (part + 1) * sb])


def fetch_pieces(copies, find, leaf, name, turns, target):
    for turn in range(turns):
        size = target.shape[1] // turns
        rows = rows_at((leaf & (turns - 1)) ^ turn, size)
        copies.start(name, find(name, turn), target.at[:, rows, :])


def finder(sources, places):
    def find(name, turn=0):
        operand, index, low, high = places[name][turn]
        source = sources[operand]
        if index is not None:
            source = source.at[index]
        return source if low is None else source.at[:, low:high, :]

    return find


def coordinates(local, per_leaf, pole, weights):
    device = lax.axis_index("wide")
    leaf, member = device // per_leaf, device % per_leaf
    return leaf, weights[member * local + pole, 0], weights[member * local + pole, 1]


def add_rows(out, rows, value, running):
    if running:
        out[rows, :] = out[rows, :] + value
    else:
        out[rows, :] = value


def send_rows(sems, first_sem, bit, per_leaf, outs, action, quarter, rows, half):
    count = rows.shape[0]
    at = (quarter % 2) * count

    def act(target):
        copy = pltpu.make_async_copy(rows, target.at[at : at + count, :], sems.at[first_sem + quarter])
        getattr(copy, action)()

    if bit:
        is_high = lax.axis_index("wide") % per_leaf & bit != 0
        pl.when(is_high)(lambda: act(outs[1 - half]))
        pl.when(jnp.logical_not(is_high))(lambda: act(outs[half]))
    else:
        act(outs[half])


def whole_kernel(sb, key, places, running, bit, *refs):
    masks, weights = refs[:2]
    sources, rest = refs[2:-20], refs[-20:]
    first_out, second_out, upper, lower, path, w1, e1, w2, e2, w3, e3, m1, m1t, m2, m2t, m3, m3t, x, x3, sems = rest
    leaf, weight_imag, weight_real = coordinates(*key, weights)
    copies = Copies(sems)
    columns = masks.shape[1]
    find = finder(sources, places)
    fetch_root(copies, find, leaf, path, sb)
    fetch_pieces(copies, find, leaf, "w_one", 4, w1)
    fetch_pieces(copies, find, leaf, "e_one", 4, e1)
    fetch_pieces(copies, find, leaf, "w_two", 2, w2)
    copies.start("w_three", find("w_three"), w3)
    fetch_pieces(copies, find, leaf, "e_two", 2, e2)
    if running:
        copies.start("upper", find("upper"), upper)
        copies.start("lower", find("lower"), lower)
    copies.start("e_three", find("e_three"), e3)
    copies.wait("root", "w_one")
    mask_panel(w1, masks, 0, m1, m1t, sb)
    couple(path, m1, x, 1, sb)
    copies.wait("e_one", "w_two")
    mask_panel(w2, masks, columns, m2, m2t, sb)
    close(path, dot(m1t[...], x[0 : 2 * sb, :]), e1, 1, sb)
    couple(path, m2, x, 2, sb)
    copies.wait("w_three", "e_two")
    mask_panel(w3, masks, 3 * columns, m3, m3t, sb)
    close(path, dot(m2t[...], x[...]), e2, 2, sb)
    if running:
        copies.wait("upper")
    for block in range(2):
        rows = slice(block * sb, (block + 1) * sb)
        product = dot(path[rows, :], m3[...])
        real, imag = product[:, 0:sb], product[:, sb : 2 * sb]
        add_rows(upper, rows, -(weight_imag * imag + weight_real * real), running)
        pack_right(x3, block * sb, real.astype(BF16), imag.astype(BF16), sb)
    send = functools.partial(send_rows, sems, copies.count, bit, key[1], (first_out, second_out))
    send("start", 0, upper.at[0:sb, :], 0)
    send("start", 1, upper.at[sb : 2 * sb, :], 0)
    if running:
        copies.wait("lower")
    product = dot(path[2 * sb :, :], m3[...])
    real, imag = product[:, 0:sb], product[:, sb : 2 * sb]
    add_rows(lower, slice(0, sb), -(weight_imag * imag + weight_real * real), running)
    pack_right(x3, 2 * sb, real.astype(BF16), imag.astype(BF16), sb)
    send("start", 2, lower.at[0:sb, :], 1)
    copies.wait("e_three")
    product = dot(m3t[...], x3[...])
    real = product[:, 0:sb] + e3[0].astype(F32)
    imag = product[:, sb : 2 * sb] + e3[1].astype(F32)
    add_rows(lower, slice(sb, 2 * sb), weight_imag * imag + weight_real * real, running)
    send("start", 3, lower.at[sb : 2 * sb, :], 1)
    send("wait", 0, upper.at[0:sb, :], 0)
    send("wait", 1, upper.at[sb : 2 * sb, :], 0)
    send("wait", 2, lower.at[0:sb, :], 1)
    send("wait", 3, lower.at[sb : 2 * sb, :], 1)


def call(kernel, name, scalars, pieces, outs, scratch, flops):
    sources, places = [], {}

    def operand(array):
        for index, known in enumerate(sources):
            if known is array:
                return index
        sources.append(array)
        return len(sources) - 1

    for key, turns in pieces.items():
        places[key] = {turn: (operand(piece[0]), *piece[1:]) for turn, piece in turns.items()}
    results = [jax.ShapeDtypeStruct(shape, kind) for shape, kind, _ in outs]
    return pl.pallas_call(
        kernel(places),
        out_shape=results,
        in_specs=[SMEM] * len(scalars) + [ANYWHERE] * len(sources),
        out_specs=[spec for _, _, spec in outs],
        scratch_shapes=[pltpu.VMEM(shape, kind) for shape, kind in scratch]
        + [pltpu.SemaphoreType.DMA((40,))],
        compiler_params=pltpu.CompilerParams(vmem_limit_bytes=60 << 20),
        cost_estimate=pl.CostEstimate(flops=flops, bytes_accessed=1 << 20, transcendentals=0),
        name=name,
    )(*scalars, *sources)


def shards(
    root_band,
    w_one,
    e_one,
    w_two,
    e_two,
    w_three,
    e_three,
    mask_one,
    mask_two,
    mask_three,
    pole_weights,
):
    devices = lax.axis_size("wide")
    per_leaf = devices // 8
    device_index = lax.axis_index("wide")
    leaf = device_index // per_leaf
    member = device_index % per_leaf
    local = root_band.shape[0]
    sb = w_three.shape[-1]
    quarter, half = sb // 4, sb // 2
    last = local - 1

    def turn(block, bits, *after):
        after = [array for array in after if array is not None]
        if after:
            block = lax.optimization_barrier((block, *after))[0]
        route = [(low, low ^ bits * per_leaf) for low in range(devices)]
        return lax.ppermute(block, "wide", route)

    early = (local + 1) // 2
    batches = [slice(0, early)] + ([slice(early, local)] if local > early else [])
    late = len(batches) > 1
    packs = [jnp.concatenate([w_one[batch], e_one[batch]], axis=2) for batch in batches]
    panels = [jnp.concatenate([w_two[pole], e_two[pole]], axis=1) for pole in range(local)]

    root = {0: root_band, 1: turn(root_band, 1)}
    root[2], root[6] = turn(root_band, 2), turn(root_band, 6)
    one = [{1: turn(packs[0], 1), 2: turn(packs[0], 2)}]
    two = []
    if last > 0:
        two.append(turn(panels[0], 1, root[1]))
    root[4] = turn(root_band, 4, root[2])
    root[7] = turn(root[1], 6, root[6])
    root[5] = turn(root[1], 4, one[0][2])
    root[3] = turn(root[1], 2, root[4])
    if late:
        one.append({1: turn(packs[1], 1, one[0][1])})
    one[0][3] = turn(one[0][1], 2, root[7])
    if last > 1:
        two.append(turn(panels[1], 1, two[0]))
    if late:
        one[1][2] = turn(packs[1], 2, root[5])
        one[1][3] = turn(one[1][1], 2, root[3])
    if last > 2:
        two.append(turn(panels[2], 1, one[1][1]))
    two.append(turn(panels[last], 1, one[0][3], *two[1:2]))

    masks = jnp.concatenate(
        [
            lax.dynamic_index_in_dim(mask_one, leaf // 4, 0, keepdims=False),
            lax.dynamic_index_in_dim(mask_two, leaf // 2, 0, keepdims=False),
            lax.dynamic_index_in_dim(mask_three, leaf, 0, keepdims=False),
        ],
        axis=0,
    )
    upper = lower = None
    single = lambda array, index=None: {0: (array, index, None, None)}
    unit = 2 * sb**3
    for pole in range(local):
        batch = 0 if pole < early else 1
        at = pole - batches[batch].start
        pieces = {"root": {bits: (root[bits], pole, None, None) for bits in range(8)}}
        pieces["w_one"], pieces["e_one"] = single(w_one, pole), single(e_one, pole)
        for bits in (1, 2, 3):
            pieces["w_one"][bits] = (one[batch][bits], at, 0, quarter)
            pieces["e_one"][bits] = (one[batch][bits], at, quarter, 2 * quarter)
        pieces["w_three"], pieces["e_three"] = single(w_three, pole), single(e_three, pole)
        key = (local, per_leaf, pole)
        running = upper is not None
        if running:
            pieces["upper"] = single(upper)
        halves = [((2 * sb, sb), F32)]
        raw = [((2, sb, sb), BF16)]
        packed = [
            ((2 * sb, 2 * sb), BF16),
            ((sb, 2 * sb), BF16),
            ((4 * sb, 2 * sb), BF16),
            ((sb, 4 * sb), BF16),
            ((6 * sb, 2 * sb), BF16),
            ((sb, 6 * sb), BF16),
            ((4 * sb, 2 * sb), BF16),
        ]
        path = [((3 * sb, 6 * sb), BF16)]
        two_raw, three_raw = [((2, 2 * sb, sb), BF16)], [((2, 3 * sb, sb), BF16)]
        pieces["w_two"] = {**single(w_two, pole), 1: (two[pole], None, 0, sb)}
        pieces["e_two"] = {**single(e_two, pole), 1: (two[pole], None, sb, sb + half)}
        if running:
            pieces["lower"] = single(lower)
        bit = per_leaf // 2 if pole == last else 0
        upper, lower = call(
            lambda places: functools.partial(whole_kernel, sb, key, places, running, bit),
            "pole_" + str(pole),
            [masks, pole_weights],
            pieces,
            [((2 * sb, sb), F32, ANYWHERE), ((2 * sb, sb), F32, ANYWHERE)],
            halves * 2 + path + raw * 2 + two_raw + raw + three_raw + raw + packed
            + [((6 * sb, 2 * sb), BF16)],
            80 * unit,
        )

    if per_leaf == 1:
        return jnp.concatenate([upper, lower], axis=0)
    bit = per_leaf // 2
    density = upper + lax.ppermute(lower, "wide", [(low, low ^ bit) for low in range(devices)])
    while bit > 1:
        bit //= 2
        half_count = density.shape[0] // 2
        bit_set = member & bit != 0
        kept = jnp.where(bit_set, density[half_count:], density[:half_count])
        sent = jnp.where(bit_set, density[:half_count], density[half_count:])
        density = kept + lax.ppermute(sent, "wide", [(low, low ^ bit) for low in range(devices)])
    return density


def solution(mesh):
    split = P(("groups", "wide"), None, None, None)
    return jax.shard_map(
        shards,
        mesh=mesh,
        in_specs=(split,) * 7 + (P("groups", None, None),) * 3 + (P(),),
        out_specs=P(("groups", "wide"), None),
        check_vma=False,
    )
```

```python
import functools

import jax
import jax.numpy as jnp
from jax import lax
from jax.experimental import pallas as pl
from jax.experimental.pallas import tpu as pltpu
from jax.sharding import PartitionSpec as P

BF16 = jnp.bfloat16
F32 = jnp.float32
SMEM = pl.BlockSpec(memory_space=pltpu.SMEM)
ANYWHERE = pl.BlockSpec(memory_space=pl.ANY)


def mask_row(masks, tile, extent, width):
    lane = lax.broadcasted_iota(jnp.int32, (1, width), 1)
    row = jnp.zeros((1, width), F32)
    for column in range(width // extent):
        value = masks[tile, column].astype(F32)
        inside = (lane >= column * extent) & (lane < (column + 1) * extent)
        row = jnp.where(inside, value, row)
    return row.astype(BF16)


def aligned(start, size):
    return pl.ds(start if isinstance(start, int) else pl.multiple_of(start, size), size)


def pack_right(target, first, real, imag, sb):
    count = real.shape[0]
    low = first + sb * (first // sb)
    target[aligned(low, count), 0:sb] = real
    target[aligned(low, count), sb : 2 * sb] = imag
    target[aligned(low + sb, count), 0:sb] = -imag
    target[aligned(low + sb, count), sb : 2 * sb] = real


def mask_panel(raw, masks, base, right, turned, sb):
    columns = masks.shape[1]
    extent = sb // columns
    blocks = raw.shape[1] // sb

    def block_step(block):
        for tile in range(columns):
            row = mask_row(masks, base + block * columns + tile, extent, sb)
            rows = aligned(block * sb + tile * extent, extent)
            real = raw[0, rows, :] * row
            imag = raw[1, rows, :] * row
            low = block * 2 * sb + tile * extent
            right[aligned(low, extent), 0:sb] = real
            right[aligned(low, extent), sb : 2 * sb] = imag
            right[aligned(low + sb, extent), 0:sb] = -imag
            right[aligned(low + sb, extent), sb : 2 * sb] = real
            turned[:, aligned(low, extent)] = real.T
            turned[:, aligned(low + sb, extent)] = imag.T

    if blocks > 2:
        pl.loop(0, blocks)(block_step)
    else:
        for block in range(blocks):
            block_step(block)


def dot(left, right):
    return jnp.dot(left, right, preferred_element_type=F32)


def couple(path, right, packed, level, sb):
    size = 2 * sb * level
    for block in range(level):
        rows = slice(block * sb, (block + 1) * sb)
        product = dot(path[rows, 0:size], right[...]).astype(BF16)
        real, imag = product[:, 0:sb], product[:, sb : 2 * sb]
        path[rows, size : size + 2 * sb] = -product
        pack_right(packed, block * sb, real, imag, sb)
        low = 2 * sb * block
        path[level * sb : (level + 1) * sb, low : low + sb] = -real.T
        path[level * sb : (level + 1) * sb, low + sb : low + 2 * sb] = -imag.T


def close(path, product, corner, level, sb):
    rows = slice(level * sb, (level + 1) * sb)
    for part in range(2):
        own = product[:, part * sb : (part + 1) * sb] + corner[part].astype(F32)
        low = 2 * sb * level + part * sb
        path[rows, low : low + sb] = own.astype(BF16)


class Copies:
    def __init__(self, sems):
        self.sems = sems
        self.started = {}
        self.count = 0

    def start(self, name, source, target):
        copy = pltpu.make_async_copy(source, target, self.sems.at[self.count])
        self.count += 1
        copy.start()
        self.started.setdefault(name, []).append(copy)

    def wait(self, *names):
        for name in names:
            for copy in self.started.pop(name):
                copy.wait()


def rows_at(index, size):
    return pl.ds(pl.multiple_of(index * size, size), size)


def fetch_root(copies, find, leaf, path, sb):
    for turn in range(8):
        rows = rows_at(leaf ^ turn, sb // 8)
        source = find("root", turn)
        for part in range(2):
            copies.start("root", source.at[part], path.at[rows, part * sb : (part + 1) * sb])


def fetch_pieces(copies, find, leaf, name, turns, target):
    for turn in range(turns):
        size = target.shape[1] // turns
        rows = rows_at((leaf & (turns - 1)) ^ turn, size)
        copies.start(name, find(name, turn), target.at[:, rows, :])


def finder(sources, places):
    def find(name, turn=0):
        operand, index, low, high = places[name][turn]
        source = sources[operand]
        if index is not None:
            source = source.at[index]
        return source if low is None else source.at[:, low:high, :]

    return find


def coordinates(local, per_leaf, pole, weights):
    device = lax.axis_index("wide")
    leaf, member = device // per_leaf, device % per_leaf
    return leaf, weights[member * local + pole, 0], weights[member * local + pole, 1]


def add_rows(out, rows, value, running):
    if running:
        out[rows, :] = out[rows, :] + value
    else:
        out[rows, :] = value


def send_rows(sems, first_sem, bit, per_leaf, outs, action, quarter, rows, half):
    count = rows.shape[0]
    at = (quarter % 2) * count

    def act(target):
        copy = pltpu.make_async_copy(rows, target.at[at : at + count, :], sems.at[first_sem + quarter])
        getattr(copy, action)()

    if bit:
        is_high = lax.axis_index("wide") % per_leaf & bit != 0
        pl.when(is_high)(lambda: act(outs[1 - half]))
        pl.when(jnp.logical_not(is_high))(lambda: act(outs[half]))
    else:
        act(outs[half])


def whole_kernel(sb, key, places, running, bit, *refs):
    masks, weights = refs[:2]
    sources, rest = refs[2:-20], refs[-20:]
    first_out, second_out, upper, lower, path, w1, e1, w2, e2, w3, e3, m1, m1t, m2, m2t, m3, m3t, x, x3, sems = rest
    leaf, weight_imag, weight_real = coordinates(*key, weights)
    copies = Copies(sems)
    columns = masks.shape[1]
    find = finder(sources, places)
    fetch_root(copies, find, leaf, path, sb)
    fetch_pieces(copies, find, leaf, "w_one", 4, w1)
    fetch_pieces(copies, find, leaf, "e_one", 4, e1)
    fetch_pieces(copies, find, leaf, "w_two", 2, w2)
    copies.start("w_three", find("w_three"), w3)
    fetch_pieces(copies, find, leaf, "e_two", 2, e2)
    if running:
        copies.start("upper", find("upper"), upper)
        copies.start("lower", find("lower"), lower)
    copies.start("e_three", find("e_three"), e3)
    copies.wait("root", "w_one")
    mask_panel(w1, masks, 0, m1, m1t, sb)
    couple(path, m1, x, 1, sb)
    copies.wait("e_one", "w_two")
    mask_panel(w2, masks, columns, m2, m2t, sb)
    close(path, dot(m1t[...], x[0 : 2 * sb, :]), e1, 1, sb)
    couple(path, m2, x, 2, sb)
    copies.wait("w_three", "e_two")
    mask_panel(w3, masks, 3 * columns, m3, m3t, sb)
    close(path, dot(m2t[...], x[...]), e2, 2, sb)
    if running:
        copies.wait("upper")
    for block in range(2):
        rows = slice(block * sb, (block + 1) * sb)
        product = dot(path[rows, :], m3[...])
        real, imag = product[:, 0:sb], product[:, sb : 2 * sb]
        add_rows(upper, rows, -(weight_imag * imag + weight_real * real), running)
        pack_right(x3, block * sb, real.astype(BF16), imag.astype(BF16), sb)
    send = functools.partial(send_rows, sems, copies.count, bit, key[1], (first_out, second_out))
    send("start", 0, upper.at[0:sb, :], 0)
    send("start", 1, upper.at[sb : 2 * sb, :], 0)
    if running:
        copies.wait("lower")
    product = dot(path[2 * sb :, :], m3[...])
    real, imag = product[:, 0:sb], product[:, sb : 2 * sb]
    add_rows(lower, slice(0, sb), -(weight_imag * imag + weight_real * real), running)
    pack_right(x3, 2 * sb, real.astype(BF16), imag.astype(BF16), sb)
    send("start", 2, lower.at[0:sb, :], 1)
    copies.wait("e_three")
    product = dot(m3t[...], x3[...])
    real = product[:, 0:sb] + e3[0].astype(F32)
    imag = product[:, sb : 2 * sb] + e3[1].astype(F32)
    add_rows(lower, slice(sb, 2 * sb), weight_imag * imag + weight_real * real, running)
    send("start", 3, lower.at[sb : 2 * sb, :], 1)
    send("wait", 0, upper.at[0:sb, :], 0)
    send("wait", 1, upper.at[sb : 2 * sb, :], 0)
    send("wait", 2, lower.at[0:sb, :], 1)
    send("wait", 3, lower.at[sb : 2 * sb, :], 1)


def call(kernel, name, scalars, pieces, outs, scratch, flops):
    sources, places = [], {}

    def operand(array):
        for index, known in enumerate(sources):
            if known is array:
                return index
        sources.append(array)
        return len(sources) - 1

    for key, turns in pieces.items():
        places[key] = {turn: (operand(piece[0]), *piece[1:]) for turn, piece in turns.items()}
    results = [jax.ShapeDtypeStruct(shape, kind) for shape, kind, _ in outs]
    return pl.pallas_call(
        kernel(places),
        out_shape=results,
        in_specs=[SMEM] * len(scalars) + [ANYWHERE] * len(sources),
        out_specs=[spec for _, _, spec in outs],
        scratch_shapes=[pltpu.VMEM(shape, kind) for shape, kind in scratch]
        + [pltpu.SemaphoreType.DMA((40,))],
        compiler_params=pltpu.CompilerParams(vmem_limit_bytes=60 << 20),
        cost_estimate=pl.CostEstimate(flops=flops, bytes_accessed=1 << 20, transcendentals=0),
        name=name,
    )(*scalars, *sources)


def shards(
    root_band,
    w_one,
    e_one,
    w_two,
    e_two,
    w_three,
    e_three,
    mask_one,
    mask_two,
    mask_three,
    pole_weights,
):
    devices = lax.axis_size("wide")
    per_leaf = devices // 8
    device_index = lax.axis_index("wide")
    leaf = device_index // per_leaf
    member = device_index % per_leaf
    local = root_band.shape[0]
    sb = w_three.shape[-1]
    quarter, half = sb // 4, sb // 2
    last = local - 1

    def turn(block, bits, *after):
        after = [array for array in after if array is not None]
        if after:
            block = lax.optimization_barrier((block, *after))[0]
        route = [(low, low ^ bits * per_leaf) for low in range(devices)]
        return lax.ppermute(block, "wide", route)

    cuts = sorted({0, min(1, local), min(2, local), local})
    batches = [slice(low, high) for low, high in zip(cuts[:-1], cuts[1:])]
    packs = [jnp.concatenate([w_one[batch], e_one[batch]], axis=2) for batch in batches]
    panels = [jnp.concatenate([w_two[pole], e_two[pole]], axis=1) for pole in range(local)]

    root = {0: root_band, 1: turn(root_band, 1)}
    root[2], root[6] = turn(root_band, 2), turn(root_band, 6)
    one = [{1: turn(packs[0], 1), 2: turn(packs[0], 2)}]
    two = [turn(panels[0], 1, root[1])]
    root[4] = turn(root_band, 4, root[2])
    root[7] = turn(root[1], 6, root[6])
    root[5] = turn(root[1], 4, one[0][2])
    root[3] = turn(root[1], 2, root[4])
    one[0][3] = turn(one[0][1], 2, root[7])
    if local > 1:
        one.append({1: turn(packs[1], 1, one[0][1])})
        two.append(turn(panels[1], 1, two[0]))
        one[1][2] = turn(packs[1], 2, root[3])
        one[1][3] = turn(one[1][1], 2, one[0][3])
    if local > 2:
        one.append({1: turn(packs[2], 1, one[1][1])})

    masks = jnp.concatenate(
        [
            lax.dynamic_index_in_dim(mask_one, leaf // 4, 0, keepdims=False),
            lax.dynamic_index_in_dim(mask_two, leaf // 2, 0, keepdims=False),
            lax.dynamic_index_in_dim(mask_three, leaf, 0, keepdims=False),
        ],
        axis=0,
    )
    upper = lower = None
    far = {}
    single = lambda array, index=None: {0: (array, index, None, None)}
    unit = 2 * sb**3
    for pole in range(local):
        batch = min(pole, 2)
        at = pole - batches[batch].start
        pieces = {"root": {bits: (root[bits], pole, None, None) for bits in range(8)}}
        pieces["w_one"], pieces["e_one"] = single(w_one, pole), single(e_one, pole)
        for bits in (1, 2, 3):
            if bits > 1 and pole in far:
                piece = (far[pole][bits], 0)
            else:
                piece = (one[batch][bits], at)
            pieces["w_one"][bits] = (*piece, 0, quarter)
            pieces["e_one"][bits] = (*piece, quarter, 2 * quarter)
        pieces["w_three"], pieces["e_three"] = single(w_three, pole), single(e_three, pole)
        key = (local, per_leaf, pole)
        running = upper is not None
        if running:
            pieces["upper"] = single(upper)
        halves = [((2 * sb, sb), F32)]
        raw = [((2, sb, sb), BF16)]
        packed = [
            ((2 * sb, 2 * sb), BF16),
            ((sb, 2 * sb), BF16),
            ((4 * sb, 2 * sb), BF16),
            ((sb, 4 * sb), BF16),
            ((6 * sb, 2 * sb), BF16),
            ((sb, 6 * sb), BF16),
            ((4 * sb, 2 * sb), BF16),
        ]
        path = [((3 * sb, 6 * sb), BF16)]
        two_raw, three_raw = [((2, 2 * sb, sb), BF16)], [((2, 3 * sb, sb), BF16)]
        pieces["w_two"] = {**single(w_two, pole), 1: (two[pole], None, 0, sb)}
        pieces["e_two"] = {**single(e_two, pole), 1: (two[pole], None, sb, sb + half)}
        if running:
            pieces["lower"] = single(lower)
        bit = per_leaf // 2 if pole == last else 0
        upper, lower = call(
            lambda places: functools.partial(whole_kernel, sb, key, places, running, bit),
            "pole_" + str(pole),
            [masks, pole_weights],
            pieces,
            [((2 * sb, sb), F32, ANYWHERE), ((2 * sb, sb), F32, ANYWHERE)],
            halves * 2 + path + raw * 2 + two_raw + raw + three_raw + raw + packed
            + [((6 * sb, 2 * sb), BF16)],
            80 * unit,
        )
        if pole < 2 and local > 2:
            for late in [2] if pole == 0 else range(3, local):
                two.append(turn(panels[late], 1, upper))
                part = slice(late - 2, late - 1)
                own, own_y = packs[2][part], one[2][1][part]
                far[late] = {2: turn(own, 2, root[5], upper), 3: turn(own_y, 2, one[1][2], upper)}

    if per_leaf == 1:
        return jnp.concatenate([upper, lower], axis=0)
    bit = per_leaf // 2
    density = upper + lax.ppermute(lower, "wide", [(low, low ^ bit) for low in range(devices)])
    while bit > 1:
        bit //= 2
        half_count = density.shape[0] // 2
        bit_set = member & bit != 0
        kept = jnp.where(bit_set, density[half_count:], density[:half_count])
        sent = jnp.where(bit_set, density[:half_count], density[half_count:])
        density = kept + lax.ppermute(sent, "wide", [(low, low ^ bit) for low in range(devices)])
    return density


def solution(mesh):
    split = P(("groups", "wide"), None, None, None)
    return jax.shard_map(
        shards,
        mesh=mesh,
        in_specs=(split,) * 7 + (P("groups", None, None),) * 3 + (P(),),
        out_specs=P(("groups", "wide"), None),
        check_vma=False,
    )
```

```python
import functools

import jax
import jax.numpy as jnp
from jax import lax
from jax.experimental import pallas as pl
from jax.experimental.pallas import tpu as pltpu
from jax.sharding import PartitionSpec as P

BF16 = jnp.bfloat16
F32 = jnp.float32
SMEM = pl.BlockSpec(memory_space=pltpu.SMEM)
ANYWHERE = pl.BlockSpec(memory_space=pl.ANY)


def mask_row(masks, tile, extent, width):
    lane = lax.broadcasted_iota(jnp.int32, (1, width), 1)
    row = jnp.zeros((1, width), F32)
    for column in range(width // extent):
        value = masks[tile, column].astype(F32)
        inside = (lane >= column * extent) & (lane < (column + 1) * extent)
        row = jnp.where(inside, value, row)
    return row.astype(BF16)


def aligned(start, size):
    return pl.ds(start if isinstance(start, int) else pl.multiple_of(start, size), size)


def pack_right(target, first, real, imag, sb):
    count = real.shape[0]
    low = first + sb * (first // sb)
    target[aligned(low, count), 0:sb] = real
    target[aligned(low, count), sb : 2 * sb] = imag
    target[aligned(low + sb, count), 0:sb] = -imag
    target[aligned(low + sb, count), sb : 2 * sb] = real


def mask_panel(raw, masks, base, right, turned, sb):
    columns = masks.shape[1]
    extent = sb // columns
    blocks = raw.shape[1] // sb

    def block_step(block):
        for tile in range(columns):
            row = mask_row(masks, base + block * columns + tile, extent, sb)
            rows = aligned(block * sb + tile * extent, extent)
            real = raw[0, rows, :] * row
            imag = raw[1, rows, :] * row
            low = block * 2 * sb + tile * extent
            right[aligned(low, extent), 0:sb] = real
            right[aligned(low, extent), sb : 2 * sb] = imag
            right[aligned(low + sb, extent), 0:sb] = -imag
            right[aligned(low + sb, extent), sb : 2 * sb] = real
            turned[:, aligned(low, extent)] = real.T
            turned[:, aligned(low + sb, extent)] = imag.T

    if blocks > 2:
        pl.loop(0, blocks)(block_step)
    else:
        for block in range(blocks):
            block_step(block)


def dot(left, right):
    return jnp.dot(left, right, preferred_element_type=F32)


def couple(path, right, packed, level, sb):
    size = 2 * sb * level
    for block in range(level):
        rows = slice(block * sb, (block + 1) * sb)
        product = dot(path[rows, 0:size], right[...]).astype(BF16)
        real, imag = product[:, 0:sb], product[:, sb : 2 * sb]
        path[rows, size : size + 2 * sb] = -product
        pack_right(packed, block * sb, real, imag, sb)
        low = 2 * sb * block
        path[level * sb : (level + 1) * sb, low : low + sb] = -real.T
        path[level * sb : (level + 1) * sb, low + sb : low + 2 * sb] = -imag.T


def close(path, product, corner, level, sb):
    rows = slice(level * sb, (level + 1) * sb)
    for part in range(2):
        own = product[:, part * sb : (part + 1) * sb] + corner[part].astype(F32)
        low = 2 * sb * level + part * sb
        path[rows, low : low + sb] = own.astype(BF16)


class Copies:
    def __init__(self, sems):
        self.sems = sems
        self.started = {}
        self.count = 0

    def start(self, name, source, target):
        copy = pltpu.make_async_copy(source, target, self.sems.at[self.count])
        self.count += 1
        copy.start()
        self.started.setdefault(name, []).append(copy)

    def wait(self, *names):
        for name in names:
            for copy in self.started.pop(name):
                copy.wait()


def rows_at(index, size):
    return pl.ds(pl.multiple_of(index * size, size), size)


def fetch_root(copies, find, leaf, path, sb):
    for turn in range(8):
        rows = rows_at(leaf ^ turn, sb // 8)
        source = find("root", turn)
        for part in range(2):
            copies.start("root", source.at[part], path.at[rows, part * sb : (part + 1) * sb])


def fetch_pieces(copies, find, leaf, name, turns, target):
    for turn in range(turns):
        size = target.shape[1] // turns
        rows = rows_at((leaf & (turns - 1)) ^ turn, size)
        copies.start(name, find(name, turn), target.at[:, rows, :])


def finder(sources, places):
    def find(name, turn=0):
        operand, index, low, high = places[name][turn]
        source = sources[operand]
        if index is not None:
            source = source.at[index]
        return source if low is None else source.at[:, low:high, :]

    return find


def coordinates(local, per_leaf, pole, weights):
    device = lax.axis_index("wide")
    leaf, member = device // per_leaf, device % per_leaf
    return leaf, weights[member * local + pole, 0], weights[member * local + pole, 1]


def add_rows(out, rows, value, running):
    if running:
        out[rows, :] = out[rows, :] + value
    else:
        out[rows, :] = value


def send_rows(sems, first_sem, bit, per_leaf, outs, action, quarter, rows, half):
    count = rows.shape[0]
    at = (quarter % 2) * count

    def act(target):
        copy = pltpu.make_async_copy(rows, target.at[at : at + count, :], sems.at[first_sem + quarter])
        getattr(copy, action)()

    if bit:
        is_high = lax.axis_index("wide") % per_leaf & bit != 0
        pl.when(is_high)(lambda: act(outs[1 - half]))
        pl.when(jnp.logical_not(is_high))(lambda: act(outs[half]))
    else:
        act(outs[half])


def whole_kernel(sb, key, places, running, bit, *refs):
    masks, weights = refs[:2]
    sources, rest = refs[2:-20], refs[-20:]
    first_out, second_out, upper, lower, path, w1, e1, w2, e2, w3, e3, m1, m1t, m2, m2t, m3, m3t, x, x3, sems = rest
    leaf, weight_imag, weight_real = coordinates(*key, weights)
    copies = Copies(sems)
    columns = masks.shape[1]
    find = finder(sources, places)
    fetch_root(copies, find, leaf, path, sb)
    fetch_pieces(copies, find, leaf, "w_one", 4, w1)
    fetch_pieces(copies, find, leaf, "e_one", 4, e1)
    fetch_pieces(copies, find, leaf, "w_two", 2, w2)
    copies.start("w_three", find("w_three"), w3)
    fetch_pieces(copies, find, leaf, "e_two", 2, e2)
    if running:
        copies.start("upper", find("upper"), upper)
        copies.start("lower", find("lower"), lower)
    copies.start("e_three", find("e_three"), e3)
    copies.wait("root", "w_one")
    mask_panel(w1, masks, 0, m1, m1t, sb)
    couple(path, m1, x, 1, sb)
    copies.wait("e_one", "w_two")
    mask_panel(w2, masks, columns, m2, m2t, sb)
    close(path, dot(m1t[...], x[0 : 2 * sb, :]), e1, 1, sb)
    couple(path, m2, x, 2, sb)
    copies.wait("w_three", "e_two")
    mask_panel(w3, masks, 3 * columns, m3, m3t, sb)
    close(path, dot(m2t[...], x[...]), e2, 2, sb)
    if running:
        copies.wait("upper")
    for block in range(2):
        rows = slice(block * sb, (block + 1) * sb)
        product = dot(path[rows, :], m3[...])
        real, imag = product[:, 0:sb], product[:, sb : 2 * sb]
        add_rows(upper, rows, -(weight_imag * imag + weight_real * real), running)
        pack_right(x3, block * sb, real.astype(BF16), imag.astype(BF16), sb)
    send = functools.partial(send_rows, sems, copies.count, bit, key[1], (first_out, second_out))
    send("start", 0, upper.at[0:sb, :], 0)
    send("start", 1, upper.at[sb : 2 * sb, :], 0)
    if running:
        copies.wait("lower")
    product = dot(path[2 * sb :, :], m3[...])
    real, imag = product[:, 0:sb], product[:, sb : 2 * sb]
    add_rows(lower, slice(0, sb), -(weight_imag * imag + weight_real * real), running)
    pack_right(x3, 2 * sb, real.astype(BF16), imag.astype(BF16), sb)
    send("start", 2, lower.at[0:sb, :], 1)
    copies.wait("e_three")
    product = dot(m3t[...], x3[...])
    real = product[:, 0:sb] + e3[0].astype(F32)
    imag = product[:, sb : 2 * sb] + e3[1].astype(F32)
    add_rows(lower, slice(sb, 2 * sb), weight_imag * imag + weight_real * real, running)
    send("start", 3, lower.at[sb : 2 * sb, :], 1)
    send("wait", 0, upper.at[0:sb, :], 0)
    send("wait", 1, upper.at[sb : 2 * sb, :], 0)
    send("wait", 2, lower.at[0:sb, :], 1)
    send("wait", 3, lower.at[sb : 2 * sb, :], 1)


def call(kernel, name, scalars, pieces, outs, scratch, flops):
    sources, places = [], {}

    def operand(array):
        for index, known in enumerate(sources):
            if known is array:
                return index
        sources.append(array)
        return len(sources) - 1

    for key, turns in pieces.items():
        places[key] = {turn: (operand(piece[0]), *piece[1:]) for turn, piece in turns.items()}
    results = [jax.ShapeDtypeStruct(shape, kind) for shape, kind, _ in outs]
    return pl.pallas_call(
        kernel(places),
        out_shape=results,
        in_specs=[SMEM] * len(scalars) + [ANYWHERE] * len(sources),
        out_specs=[spec for _, _, spec in outs],
        scratch_shapes=[pltpu.VMEM(shape, kind) for shape, kind in scratch]
        + [pltpu.SemaphoreType.DMA((40,))],
        compiler_params=pltpu.CompilerParams(vmem_limit_bytes=60 << 20),
        cost_estimate=pl.CostEstimate(flops=flops, bytes_accessed=1 << 20, transcendentals=0),
        name=name,
    )(*scalars, *sources)


def shards(
    root_band,
    w_one,
    e_one,
    w_two,
    e_two,
    w_three,
    e_three,
    mask_one,
    mask_two,
    mask_three,
    pole_weights,
):
    devices = lax.axis_size("wide")
    per_leaf = devices // 8
    device_index = lax.axis_index("wide")
    leaf = device_index // per_leaf
    member = device_index % per_leaf
    local = root_band.shape[0]
    sb = w_three.shape[-1]
    quarter, half = sb // 4, sb // 2
    last = local - 1

    def turn(block, bits, *after):
        after = [array for array in after if array is not None]
        if after:
            block = lax.optimization_barrier((block, *after))[0]
        route = [(low, low ^ bits * per_leaf) for low in range(devices)]
        return lax.ppermute(block, "wide", route)

    cuts = sorted({0, min(1, local), min(2, local), local})
    batches = [slice(low, high) for low, high in zip(cuts[:-1], cuts[1:])]
    packs = [jnp.concatenate([w_one[batch], e_one[batch]], axis=2) for batch in batches]
    panels = [jnp.concatenate([w_two[pole], e_two[pole]], axis=1) for pole in range(local)]

    root = {0: root_band, 1: turn(root_band, 1)}
    root[2], root[6] = turn(root_band, 2), turn(root_band, 6)
    one = [{1: turn(packs[0], 1), 2: turn(packs[0], 2)}]
    two = [turn(panels[0], 1, root[1])]
    root[4] = turn(root_band, 4, root[2])
    root[7] = turn(root[1], 6, root[6])
    one[0][3] = turn(one[0][1], 2, one[0][2])
    root[5] = turn(root[1], 4, one[0][3])
    root[3] = turn(root[1], 2, root[4])
    if local > 1:
        one.append({1: turn(packs[1], 1, one[0][1])})
        two.append(turn(panels[1], 1, two[0]))
        one[1][2] = turn(packs[1], 2, root[3])
        one[1][3] = turn(one[1][1], 2, root[7])
    if local > 2:
        one.append({1: turn(packs[2], 1, one[1][1])})

    masks = jnp.concatenate(
        [
            lax.dynamic_index_in_dim(mask_one, leaf // 4, 0, keepdims=False),
            lax.dynamic_index_in_dim(mask_two, leaf // 2, 0, keepdims=False),
            lax.dynamic_index_in_dim(mask_three, leaf, 0, keepdims=False),
        ],
        axis=0,
    )
    upper = lower = None
    far = {}
    single = lambda array, index=None: {0: (array, index, None, None)}
    unit = 2 * sb**3
    for pole in range(local):
        batch = min(pole, 2)
        at = pole - batches[batch].start
        pieces = {"root": {bits: (root[bits], pole, None, None) for bits in range(8)}}
        pieces["w_one"], pieces["e_one"] = single(w_one, pole), single(e_one, pole)
        for bits in (1, 2, 3):
            if bits > 1 and pole in far:
                piece = (far[pole][bits], 0)
            else:
                piece = (one[batch][bits], at)
            pieces["w_one"][bits] = (*piece, 0, quarter)
            pieces["e_one"][bits] = (*piece, quarter, 2 * quarter)
        pieces["w_three"], pieces["e_three"] = single(w_three, pole), single(e_three, pole)
        key = (local, per_leaf, pole)
        running = upper is not None
        if running:
            pieces["upper"] = single(upper)
        halves = [((2 * sb, sb), F32)]
        raw = [((2, sb, sb), BF16)]
        packed = [
            ((2 * sb, 2 * sb), BF16),
            ((sb, 2 * sb), BF16),
            ((4 * sb, 2 * sb), BF16),
            ((sb, 4 * sb), BF16),
            ((6 * sb, 2 * sb), BF16),
            ((sb, 6 * sb), BF16),
            ((4 * sb, 2 * sb), BF16),
        ]
        path = [((3 * sb, 6 * sb), BF16)]
        two_raw, three_raw = [((2, 2 * sb, sb), BF16)], [((2, 3 * sb, sb), BF16)]
        pieces["w_two"] = {**single(w_two, pole), 1: (two[pole], None, 0, sb)}
        pieces["e_two"] = {**single(e_two, pole), 1: (two[pole], None, sb, sb + half)}
        if running:
            pieces["lower"] = single(lower)
        bit = per_leaf // 2 if pole == last else 0
        upper, lower = call(
            lambda places: functools.partial(whole_kernel, sb, key, places, running, bit),
            "pole_" + str(pole),
            [masks, pole_weights],
            pieces,
            [((2 * sb, sb), F32, ANYWHERE), ((2 * sb, sb), F32, ANYWHERE)],
            halves * 2 + path + raw * 2 + two_raw + raw + three_raw + raw + packed
            + [((6 * sb, 2 * sb), BF16)],
            80 * unit,
        )
        if pole < 2 and local > 2:
            for late in [2] if pole == 0 else range(3, local):
                two.append(turn(panels[late], 1, upper))
                part = slice(late - 2, late - 1)
                own, own_y = packs[2][part], one[2][1][part]
                far[late] = {2: turn(own, 2, root[5], upper), 3: turn(own_y, 2, one[1][2], upper)}

    if per_leaf == 1:
        return jnp.concatenate([upper, lower], axis=0)
    bit = per_leaf // 2
    density = upper + lax.ppermute(lower, "wide", [(low, low ^ bit) for low in range(devices)])
    while bit > 1:
        bit //= 2
        half_count = density.shape[0] // 2
        bit_set = member & bit != 0
        kept = jnp.where(bit_set, density[half_count:], density[:half_count])
        sent = jnp.where(bit_set, density[:half_count], density[half_count:])
        density = kept + lax.ppermute(sent, "wide", [(low, low ^ bit) for low in range(devices)])
    return density


def solution(mesh):
    split = P(("groups", "wide"), None, None, None)
    return jax.shard_map(
        shards,
        mesh=mesh,
        in_specs=(split,) * 7 + (P("groups", None, None),) * 3 + (P(),),
        out_specs=P(("groups", "wide"), None),
        check_vma=False,
    )
```
